32 devices in a mesh: design: 2 (over x), pts: 16 (over z, y, core).
Axes of the slice: x: 2, y: 2, z: 4, core: 2. Of those that a mesh axis runs over, the one named last changes fastest.
Arguments:
- points: bfloat16 [8192, 256], P(('design', 'pts')), parts along dimension 0, may hold values from -6 to 6
- geometry: bfloat16 [16384, 256], P(('design', 'pts')), parts along dimension 0, may hold values from -6 to 6
- counts: int32 [32], P(('design', 'pts')), parts along dimension 0, may hold values from 128 to 256, as said below
- cotangent: bfloat16 [8192, 256], P(('design', 'pts')), parts along dimension 0, may hold values from -0.09375 to 0.09375
- gain_attn: float32 [256], replicated, may hold values from 0.5 to 1.5
- w_feat: bfloat16 [256, 256], replicated, may hold values from -0.375 to 0.375
- w_mid: bfloat16 [256, 256], replicated, may hold values from -0.375 to 0.375
- w_slice: bfloat16 [32, 256], replicated, may hold values from -1 to 1
- sharpness: float32 [8], replicated, may hold values from 0.5 to 6
- w_query: float32 [32, 32], replicated, may hold values from -0.5 to 0.5
- w_key: float32 [32, 32], replicated, may hold values from -0.5 to 0.5
- w_value: float32 [32, 32], replicated, may hold values from -1 to 1
- w_out: bfloat16 [256, 256], replicated, may hold values from -0.375 to 0.375
- gain_mlp: float32 [256], replicated, may hold values from 0.5 to 1.5
- w_up: bfloat16 [256, 1024], replicated, may hold values from -0.375 to 0.375
- w_down: bfloat16 [1024, 256], replicated, may hold values from -0.1875 to 0.1875
Outputs:
- layer_out: bfloat16 [8192, 256], P(('design', 'pts')), parts along dimension 0
- grad_feat: float32 [512, 256], P(('design', 'pts')), parts along dimension 0
- grad_mid: float32 [512, 256], P(('design', 'pts')), parts along dimension 0
- grad_out: float32 [512, 256], P(('design', 'pts')), parts along dimension 0
- grad_up: float32 [512, 1024], P(('design', 'pts')), parts along dimension 0
- grad_down: float32 [2048, 256], P(('design', 'pts')), parts along dimension 0
- grad_slice: float32 [64, 256], P('design'), parts along dimension 0
- grad_mix: float32 [6, 32, 32], P('design'), parts along dimension 0
The draws below stay inside these ranges and needn't reach their ends.
There are 2 independent parts, one for each index of `design`. The reference program is written for one: setup_inputs(seed, part) draws one part's arguments, and reference() takes and returns one part's arrays. A program takes and returns all parts, laid end to end along the dimension named above; an argument that names none is the same for every part. Nothing has to cross between parts.
Inputs may be any that keep to these rules, and one draw needn't show every extreme that they name: `counts`: every device of a design holds at least half of its 256 slots live, and some device holds all of them.
All inputs are finite; a program needn't handle non-finite values.
Results may differ from the reference program's by a relative error of at most 0.017.
The reference program's roundings to bfloat16 on the way (of `mixed_low`, `attended`, `second_low`, `hidden`, `grad_upper`, `grad_resid` and `grad_att`) count: a program that leaves them out, or rounds other values in their place, can miss the bound.
Values sent between devices are 32-bit elements; how exact they have to be, the bound alone decides.
No kernel may reach another device: no remote copies, remote signals or barrier semaphores. Data moves between devices by JAX's collectives and lax.ppermute only.
A program may use at most 64 MiB of HBM per device.

```python
import math
import jax
import jax.numpy as jnp
from jax import lax

D = 256
HEADS = 8
DH = 32
SLICES = 256
FF = 1024
P_DEV = 256
POINTS = 4096
GEO_POINTS = 8192
N_PTS = 16


def draw_counts(key, part):
    level_key = jax.random.fold_in(key, 11)
    pick_key = jax.random.fold_in(key, 12)
    levels = jax.random.randint(level_key, (N_PTS,), P_DEV // 2, P_DEV + 1)
    chosen = jax.random.randint(pick_key, (), 0, N_PTS)
    return jnp.where(jnp.arange(N_PTS) == chosen, P_DEV, levels).astype(jnp.int32)


def draw_sharpness(key, part):
    base = jax.random.uniform(jax.random.fold_in(key, 21), (HEADS,), jnp.float32, math.log(0.5), math.log(4.0))
    return jnp.exp(base).astype(jnp.float32)


def draw_points(key, part):
    noise_key = jax.random.fold_in(key, 31)
    scale_key = jax.random.fold_in(key, 32)
    noise = jnp.clip(jax.random.normal(noise_key, (POINTS, D), jnp.float32), -6.0, 6.0)
    scales = jnp.exp(jax.random.uniform(scale_key, (POINTS, 1), jnp.float32, math.log(1.0 / 32.0), math.log(1.0 / 12.0)))
    return (noise * scales).astype(jnp.bfloat16)


def block_levels(rng, dims, cuts, least, top_value):
    def one(axis_at, shards_of):
        steps = jax.random.uniform(jax.random.fold_in(jax.random.fold_in(rng, 6), axis_at), (shards_of,), jnp.float32, least / len(cuts), top_value / len(cuts))
        return jnp.repeat(jnp.exp(steps), dims[axis_at] // shards_of).reshape((-1,) + (1,) * (len(dims) - axis_at - 1))

    level = one(*cuts[0])
    for cut in cuts[1:]:
        level = level * one(*cut)
    return level


def normal_values(key, extent, scale, limit, cuts=(), kind=jnp.bfloat16):
    result = scale * jax.random.normal(key, extent, jnp.float32)
    if cuts:
        result = result * block_levels(key, extent, cuts, -0.22, 0.18)
    return jnp.clip(result, -limit, limit).astype(kind)


def setup_inputs(seed: int = 0, part: int = 0) -> dict:
    key_list = jax.random.split(jax.random.key(seed), 17)
    part_keys = jax.random.split(jax.random.fold_in(key_list[16], part), 17)
    points = draw_points(jax.random.fold_in(jax.random.fold_in(key_list[16], part), 71), part)
    geometry = normal_values(part_keys[1], (GEO_POINTS, D), 1.0, 6.0, ((0, 16),))
    counts = draw_counts(jax.random.fold_in(jax.random.fold_in(key_list[16], part), 71), part)
    cotangent = normal_values(part_keys[3], (POINTS, D), ((P_DEV * N_PTS) ** -0.5), 0.09375, ((0, 16),))
    gain_attn = jnp.clip(1.0 + 0.1 * jax.random.normal(key_list[4], (D,), jnp.float32), 0.5, 1.5)
    w_feat = normal_values(key_list[5], (D, D), D ** -0.5, 0.375)
    w_mid = normal_values(key_list[6], (D, D), D ** -0.5, 0.375)
    w_slice = normal_values(key_list[7], (DH, SLICES), DH ** -0.5, 1.0)
    sharpness = draw_sharpness(jax.random.fold_in(key_list[16], 71), part)
    w_query = normal_values(key_list[9], (DH, DH), (DH * 4) ** -0.5, 0.5, (), jnp.float32)
    w_key = normal_values(key_list[10], (DH, DH), (DH * 4) ** -0.5, 0.5, (), jnp.float32)
    w_value = normal_values(key_list[11], (DH, DH), DH ** -0.5, 1.0, (), jnp.float32)
    w_out = normal_values(key_list[12], (D, D), D ** -0.5, 0.375)
    gain_mlp = jnp.clip(1.0 + 0.1 * jax.random.normal(key_list[13], (D,), jnp.float32), 0.5, 1.5)
    w_up = normal_values(key_list[14], (D, FF), D ** -0.5, 0.375)
    w_down = normal_values(key_list[15], (FF, D), FF ** -0.5, 0.1875)
    return dict(points=points, geometry=geometry, counts=counts, cotangent=cotangent, gain_attn=gain_attn, w_feat=w_feat, w_mid=w_mid, w_slice=w_slice, sharpness=sharpness, w_query=w_query, w_key=w_key, w_value=w_value, w_out=w_out, gain_mlp=gain_mlp, w_up=w_up, w_down=w_down)


def layer_norm(inputs, gain):
    inputs = inputs.astype(jnp.float32)
    centre = lax.optimization_barrier(jnp.mean(inputs, axis=-1, keepdims=True))
    shifted = inputs - centre
    spread = lax.optimization_barrier(jnp.mean(shifted * shifted, axis=-1, keepdims=True))
    return shifted * lax.rsqrt(spread + 1e-05) * gain

def gelu_tanh(inputs):
    return jax.nn.gelu(inputs, approximate=True)

def project(inputs, gain_attn, w_feat, w_mid):
    normed = layer_norm(inputs, gain_attn).astype(jnp.bfloat16)
    features = jnp.dot(normed, w_feat, preferred_element_type=jnp.float32).astype(jnp.bfloat16)
    middle = jnp.dot(normed, w_mid, preferred_element_type=jnp.float32).astype(jnp.bfloat16)
    return (normed, features, middle)

def slice_shares(middle, w_slice, sharpness):
    count = middle.shape[0]
    heads = sharpness.shape[0]
    logits = jnp.dot(middle.reshape(count * heads, -1), w_slice, preferred_element_type=jnp.float32)
    logits = logits.reshape(count, heads, -1) * sharpness[None, :, None]
    largest = lax.optimization_barrier(jnp.max(logits, axis=-1, keepdims=True))
    powers = jnp.exp(logits - largest)
    return powers / lax.optimization_barrier(jnp.sum(powers, axis=-1, keepdims=True))

def mix_tokens(numerator, denominator, geo_numerator, geo_denominator, w_query, w_key, w_value):
    highest = lax.Precision.HIGHEST
    field_tokens = numerator / (denominator + 1e-05)[:, :, None]
    geo_tokens = geo_numerator / (geo_denominator + 1e-05)[:, :, None]
    both = jnp.concatenate([field_tokens, geo_tokens], axis=1)
    query = jnp.einsum('hme,ef->hmf', field_tokens, w_query, precision=highest)
    key_rows = jnp.einsum('hke,ef->hkf', both, w_key, precision=highest)
    value_rows = jnp.einsum('hke,ef->hkf', both, w_value, precision=highest)
    scores = jnp.einsum('hmf,hkf->hmk', query, key_rows, precision=highest) / math.sqrt(w_query.shape[0])
    largest = lax.optimization_barrier(jnp.max(scores, axis=-1, keepdims=True))
    powers = jnp.exp(scores - largest)
    attention = powers / lax.optimization_barrier(jnp.sum(powers, axis=-1, keepdims=True))
    return jnp.einsum('hmk,hkf->hmf', attention, value_rows, precision=highest)

def mlp_pass(inputs, seed_block, weights_low, mixed_low, w_out, gain_mlp, w_up, w_down):
    count, heads, slices = weights_low.shape
    attended = jnp.einsum('bhm,hme->bhe', weights_low.astype(jnp.float32), mixed_low.astype(jnp.float32))
    attended = attended.reshape(count, -1).astype(jnp.bfloat16)
    residual = inputs.astype(jnp.float32) + jnp.dot(attended, w_out, preferred_element_type=jnp.float32)

    def mlp_norm(values_in):
        return layer_norm(values_in, gain_mlp)
    second, norm_back = jax.vjp(mlp_norm, residual)
    second_low = second.astype(jnp.bfloat16)
    upper = jnp.dot(second_low, w_up, preferred_element_type=jnp.float32)
    active, gelu_back = jax.vjp(gelu_tanh, upper)
    hidden = active.astype(jnp.bfloat16)
    layer_block = (residual + jnp.dot(hidden, w_down, preferred_element_type=jnp.float32)).astype(jnp.bfloat16)
    grad_hidden = jnp.dot(seed_block, w_down.T, preferred_element_type=jnp.float32)
    grad_upper = gelu_back(grad_hidden)[0].astype(jnp.bfloat16)
    grad_second = jnp.dot(grad_upper, w_up.T, preferred_element_type=jnp.float32)
    grad_resid = (seed_block.astype(jnp.float32) + norm_back(grad_second)[0]).astype(jnp.bfloat16)
    grad_att = jnp.dot(grad_resid, w_out.T, preferred_element_type=jnp.float32).astype(jnp.bfloat16)
    return (layer_block, attended, second_low, hidden, grad_upper, grad_resid, grad_att)

def point_back(shares, valid, weights_low, features, grad_att, mixed_low, numer_low, denom_grad, sharpness):
    count, heads, slices = shares.shape
    feats = features.reshape(count, heads, -1).astype(jnp.float32)
    grad_weights = jnp.einsum('bhe,hme->bhm', feats, numer_low.astype(jnp.float32)) + denom_grad[None]
    if grad_att is not None:
        grad_weights = grad_weights + jnp.einsum('bhe,hme->bhm', grad_att.reshape(count, heads, -1).astype(jnp.float32), mixed_low.astype(jnp.float32))
    grad_weights = grad_weights * valid[:, None, None]
    inner = lax.optimization_barrier(jnp.sum(shares * grad_weights, axis=-1, keepdims=True))
    logit_low = (shares * (grad_weights - inner) * sharpness[None, :, None]).astype(jnp.bfloat16)
    grad_features = jnp.einsum('bhm,hme->bhe', weights_low.astype(jnp.float32), numer_low.astype(jnp.float32))
    grad_features = grad_features.reshape(count, -1).astype(jnp.bfloat16)
    return (logit_low, grad_features)

def middle_back(logit_low, middle, w_slice):
    count, heads, slices = logit_low.shape
    flat = logit_low.reshape(count * heads, slices)
    grad_middle = jnp.dot(flat, w_slice.T, preferred_element_type=jnp.float32).reshape(count, -1).astype(jnp.bfloat16)
    slice_term = jnp.dot(middle.reshape(count * heads, -1).T, flat, preferred_element_type=jnp.float32)
    return (grad_middle, slice_term)

def reference(points, geometry, counts, cotangent, gain_attn, w_feat, w_mid, w_slice, sharpness, w_query, w_key, w_value, w_out, gain_mlp, w_up, w_down):
    total = points.shape[0]
    index = jnp.arange(total, dtype=jnp.int32)
    valid = (index % P_DEV < counts[index // P_DEV]).astype(jnp.float32)
    geo_valid = jnp.ones((geometry.shape[0],), jnp.float32)

    def forward_sums(inputs, keep):
        block = math.gcd(inputs.shape[0], 512)

        def step(carry, pieces):
            rows_in, keep_block = pieces
            normed, features, middle = project(rows_in, gain_attn, w_feat, w_mid)
            shares = slice_shares(middle, w_slice, sharpness)
            weights = shares * keep_block[:, None, None]
            weights_low = weights.astype(jnp.bfloat16)
            numerator = jnp.einsum('bhm,bhe->hme', weights_low.astype(jnp.float32), features.reshape(block, HEADS, DH).astype(jnp.float32))
            return ((carry[0] + numerator, carry[1] + lax.optimization_barrier(jnp.sum(weights, axis=0))), None)
        start = (jnp.zeros((HEADS, SLICES, DH), jnp.float32), jnp.zeros((HEADS, SLICES), jnp.float32))
        sums, _ = lax.scan(step, start, (inputs.reshape(-1, block, D), keep.reshape(-1, block)))
        return sums
    field_sums = forward_sums(points, valid)
    geo_sums = forward_sums(geometry, geo_valid)
    mixed, token_back = jax.vjp(mix_tokens, field_sums[0], field_sums[1], geo_sums[0], geo_sums[1], w_query, w_key, w_value)
    mixed_low = mixed.astype(jnp.bfloat16)
    block = math.gcd(total, 512)

    def mlp_step(carry, pieces):
        rows_in, keep_block, seed_block = pieces
        normed, features, middle = project(rows_in, gain_attn, w_feat, w_mid)
        shares = slice_shares(middle, w_slice, sharpness)
        weights_low = (shares * keep_block[:, None, None]).astype(jnp.bfloat16)
        layer_block, attended, second_low, hidden, grad_upper, grad_resid, grad_att = mlp_pass(rows_in, seed_block, weights_low, mixed_low, w_out, gain_mlp, w_up, w_down)
        down_acc, up_acc, out_acc, mixed_acc = carry
        down_acc = down_acc + jnp.dot(hidden.T, seed_block, preferred_element_type=jnp.float32)
        up_acc = up_acc + jnp.dot(second_low.T, grad_upper, preferred_element_type=jnp.float32)
        out_acc = out_acc + jnp.dot(attended.T, grad_resid, preferred_element_type=jnp.float32)
        mixed_acc = mixed_acc + jnp.einsum('bhm,bhe->hme', weights_low.astype(jnp.float32), grad_att.reshape(block, HEADS, DH).astype(jnp.float32))
        return ((down_acc, up_acc, out_acc, mixed_acc), (layer_block, grad_att))
    start = (jnp.zeros((FF, D), jnp.float32), jnp.zeros((D, FF), jnp.float32), jnp.zeros((D, D), jnp.float32), jnp.zeros((HEADS, SLICES, DH), jnp.float32))
    accum, outputs = lax.scan(mlp_step, start, (points.reshape(-1, block, D), valid.reshape(-1, block), cotangent.reshape(-1, block, D)))
    grad_down, grad_up, grad_out, mixed_grad = accum
    layer_out = outputs[0].reshape(total, D)
    grad_att_all = outputs[1]
    grads = token_back(mixed_grad)
    numer_low = grads[0].astype(jnp.bfloat16)
    geo_numer_low = grads[2].astype(jnp.bfloat16)
    grad_mix = jnp.stack([grads[4], grads[5], grads[6]])

    def back_sums(inputs, keep, att_blocks, numer_use, denom_use):
        size = math.gcd(inputs.shape[0], 512)

        def step(carry, pieces):
            rows_in, keep_block, att_block = pieces
            normed, features, middle = project(rows_in, gain_attn, w_feat, w_mid)
            shares = slice_shares(middle, w_slice, sharpness)
            weights_low = (shares * keep_block[:, None, None]).astype(jnp.bfloat16)
            logit_low, grad_features = point_back(shares, keep_block, weights_low, features, att_block, mixed_low, numer_use, denom_use, sharpness)
            grad_middle, slice_term = middle_back(logit_low, middle, w_slice)
            feat_acc, mid_acc, slice_acc = carry
            feat_acc = feat_acc + jnp.dot(normed.T, grad_features, preferred_element_type=jnp.float32)
            mid_acc = mid_acc + jnp.dot(normed.T, grad_middle, preferred_element_type=jnp.float32)
            return ((feat_acc, mid_acc, slice_acc + slice_term), None)
        if att_blocks is None:

            def plain_step(carry, pieces):
                return step(carry, (pieces[0], pieces[1], None))
            scan_fn = plain_step
            scanned = (inputs.reshape(-1, size, D), keep.reshape(-1, size))
        else:
            scan_fn = step
            scanned = (inputs.reshape(-1, size, D), keep.reshape(-1, size), att_blocks)
        init = (jnp.zeros((D, D), jnp.float32), jnp.zeros((D, D), jnp.float32), jnp.zeros((DH, SLICES), jnp.float32))
        sums, _ = lax.scan(scan_fn, init, scanned)
        return sums
    field_back = back_sums(points, valid, grad_att_all, numer_low, grads[1])
    geo_back = back_sums(geometry, geo_valid, None, geo_numer_low, grads[3])
    grad_feat = field_back[0] + geo_back[0]
    grad_mid = field_back[1] + geo_back[1]
    grad_slice = field_back[2] + geo_back[2]
    return (layer_out, grad_feat, grad_mid, grad_out, grad_up, grad_down, grad_slice, grad_mix)
```

```python
import functools
import math

import jax
import jax.numpy as jnp
from jax import lax
from jax.experimental import pallas as pl
from jax.experimental.pallas import tpu as pltpu
from jax.sharding import PartitionSpec as P

F32 = jnp.float32
BF16 = jnp.bfloat16
HIGHEST = lax.Precision.HIGHEST
EPS = 1e-05
GROUP_BITS = 2
GELU_A = math.sqrt(2.0 / math.pi)
GELU_B = 0.044715

NN = ((1,), (0,))
NT = ((1,), (1,))
TN = ((0,), (0,))


def dot(left, right, dims=NN, precision=None):
    return lax.dot_general(
        left, right, (dims, ((), ())), precision=precision, preferred_element_type=F32
    )


def bit_reverse(value, bits):
    out = 0
    for k in range(bits):
        out = (out << 1) | ((value >> k) & 1)
    return out


def norm_parts(inputs):
    centre = jnp.mean(inputs, axis=-1, keepdims=True)
    shifted = inputs - centre
    spread = jnp.mean(shifted * shifted, axis=-1, keepdims=True)
    return shifted, lax.rsqrt(spread + EPS)


def pad_to(count, unit):
    return -(-count // unit) * unit


def spread_heads(ref, heads, width, slices, block_of):
    ref[...] = jnp.zeros_like(ref)
    for h in range(heads):
        ref[h * width : (h + 1) * width, h * slices : (h + 1) * slices] = block_of(h).astype(BF16)


def sums_kernel(
    counts,
    sharpness,
    points,
    geometry,
    gain,
    w_feat,
    w_mid,
    w_slice,
    keep,
    send,
    normed_out,
    features_out,
    middle_t_out,
    weights_out,
    total,
    slice_map,
):
    me = lax.axis_index("pts")
    rows, model = points.shape
    width, slices = w_slice.shape
    heads = model // width
    groups = total.shape[0]
    per = heads // groups
    bits = groups.bit_length() - 1
    spread_heads(slice_map, heads, width, slices, lambda h: w_slice[...])
    total[...] = jnp.zeros_like(total)
    gain_row = gain[...].reshape(1, model)

    def block(inputs, at, geo):
        shifted, scale = norm_parts(inputs.astype(F32))
        normed = (shifted * scale * gain_row).astype(BF16)
        features = dot(normed, w_feat[...]).astype(BF16)
        middle = dot(normed, w_mid[...]).astype(BF16)
        features_t = features.T
        normed_out[at, :] = normed
        features_out[at, :] = features
        middle_t_out[:, at] = middle.T
        if not geo:
            live = lax.broadcasted_iota(jnp.int32, (rows, 1), 0) < counts[0]
        for h in range(heads):
            cols = slice(h * slices, (h + 1) * slices)
            logits = dot(middle, slice_map[:, cols]) * sharpness[h]
            powers = jnp.exp(logits - jnp.max(logits, axis=1, keepdims=True))
            inverse = 1.0 / jnp.sum(powers, axis=1, keepdims=True)
            if not geo:
                inverse = jnp.where(live, inverse, 0.0)
            weights = powers * inverse
            weights_out[at, cols] = weights
            g, j = h // per, h % per
            num_row = (int(geo) * per + j) * width
            den_row = 2 * per * width + int(geo) * per + j
            total[g, num_row : num_row + width, :] += dot(
                features_t[h * width : (h + 1) * width], weights.astype(BF16)
            )
            total[g, den_row : den_row + 1, :] += jnp.sum(weights, axis=0, keepdims=True)

    block(points[...], pl.ds(0, rows), False)

    @pl.loop(0, geometry.shape[0] // rows)
    def _(i):
        start = pl.multiple_of(i * rows, rows)
        block(geometry[pl.ds(start, rows), :], pl.ds(pl.multiple_of(start + rows, rows), rows), True)

    for pos in range(groups):
        value = total[bit_reverse(pos, bits) ^ (me & (groups - 1))]
        if pos < groups // 2:
            keep[pos] = value
        else:
            send[pos - groups // 2] = value


def token_rows(tokens, j, per, width):
    base = 2 * per * width
    out = []
    for geo in range(2):
        row = (geo * per + j) * width
        den = tokens[base + geo * per + j : base + geo * per + j + 1, :] + EPS
        out.append((tokens[row : row + width, :] / den, den))
    return out


def mix_kernel(tokens, w_query, w_key, w_value, mixed_out, attention_out):
    width = w_query.shape[0]
    per = attention_out.shape[0]
    for j in range(per):
        (field, _), (geo, _) = token_rows(tokens, j, per, width)
        both = jnp.concatenate([field, geo], axis=1)
        query = dot(w_query[...], field, TN, HIGHEST)
        keys = dot(w_key[...], both, TN, HIGHEST)
        values = dot(w_value[...], both, TN, HIGHEST)
        scores = dot(keys, query, TN, HIGHEST) / math.sqrt(width)
        powers = jnp.exp(scores - jnp.max(scores, axis=0, keepdims=True))
        attention = powers * (1.0 / jnp.sum(powers, axis=0, keepdims=True))
        attention_out[j] = attention
        mixed_out[j * width : (j + 1) * width, :] = dot(values, attention, NN, HIGHEST)


def mix_back_kernel(tokens, attention_in, grad, w_query, w_key, w_value, out):
    width = w_query.shape[0]
    per, both_count, slices = attention_in.shape
    base = 2 * per * width
    small = jnp.zeros((width, 3 * width), F32)
    out[base : base + 8 * pl.cdiv(2 * per, 8), :] = jnp.zeros((8 * pl.cdiv(2 * per, 8), slices), F32)
    for j in range(per):
        (field, field_den), (geo, geo_den) = token_rows(tokens, j, per, width)
        both = jnp.concatenate([field, geo], axis=1)
        query = dot(w_query[...], field, TN, HIGHEST)
        keys = dot(w_key[...], both, TN, HIGHEST)
        values = dot(w_value[...], both, TN, HIGHEST)
        attention = attention_in[j]
        mixed_grad = grad[j * width : (j + 1) * width, :]
        att_grad = dot(values, mixed_grad, TN, HIGHEST)
        inner = jnp.sum(attention * att_grad, axis=0, keepdims=True)
        score_grad = attention * (att_grad - inner) * (1.0 / math.sqrt(width))
        value_grad = dot(mixed_grad, attention, NT, HIGHEST)
        query_grad = dot(keys, score_grad, NN, HIGHEST)
        key_grad = dot(query, score_grad, NT, HIGHEST)
        both_grad = dot(w_key[...], key_grad, NN, HIGHEST) + dot(
            w_value[...], value_grad, NN, HIGHEST
        )
        field_grad = both_grad[:, :slices] + dot(w_query[...], query_grad, NN, HIGHEST)
        geo_grad = both_grad[:, slices:]
        small += jnp.concatenate(
            [
                dot(field, query_grad, NT, HIGHEST),
                dot(both, key_grad, NT, HIGHEST),
                dot(both, value_grad, NT, HIGHEST),
            ],
            axis=1,
        )
        for g, (value, den, value_of) in enumerate(
            ((field_grad, field_den, field), (geo_grad, geo_den, geo))
        ):
            row = (g * per + j) * width
            scaled = value / den
            out[row : row + width, :] = scaled
            out[base + g * per + j : base + g * per + j + 1, :] = -jnp.sum(
                scaled * value_of, axis=0, keepdims=True
            )
    half = width // 2
    filler = jnp.zeros((width, slices // 2 - 3 * width), F32)
    wide = jnp.concatenate([small, filler], axis=1)
    out[out.shape[0] - half :, :] = jnp.concatenate([wide[:half], wide[half:]], axis=1)


def mlp_kernel(
    rel,
    *refs,
):
    groups = len(rel)
    pieces = refs[:groups]
    (
        weights,
        points,
        cotangent,
        w_out,
        gain,
        w_up,
        w_down,
        layer_out,
        grad_att_out,
        keep,
        send,
        attended_out,
        second_out,
        hidden_out,
        grad_upper_out,
        grad_resid_out,
        canon,
        mix_map,
    ) = refs[groups:]
    me = lax.axis_index("pts")
    model = points.shape[1]
    slices = canon.shape[2]
    heads = weights.shape[1] // slices
    width = model // heads
    per = heads // groups
    bits = groups.bit_length() - 1
    mine = me & (groups - 1)
    for r, piece in zip(rel, pieces):
        canon[mine ^ r] = piece[...]
    spread_heads(
        mix_map,
        heads,
        width,
        slices,
        lambda h: canon[h // per, (h % per) * width : (h % per + 1) * width, :],
    )
    gain_row = gain[...].reshape(1, model)
    weights_low = weights[...].astype(BF16)
    attended = dot(weights_low, mix_map[...], NT).astype(BF16)
    attended_out[...] = attended
    residual = points[...].astype(F32) + dot(attended, w_out[...])
    shifted, scale = norm_parts(residual)
    unit = shifted * scale
    second = (unit * gain_row).astype(BF16)
    second_out[...] = second
    upper = dot(second, w_up[...])
    square = upper * upper
    slope = jnp.tanh(GELU_A * upper * (1.0 + GELU_B * square))
    half = 0.5 * (1.0 + slope)
    hidden = (upper * half).astype(BF16)
    hidden_out[...] = hidden
    curve = half + 0.5 * upper * (1.0 - slope * slope) * (
        GELU_A * (1.0 + 3.0 * GELU_B * square)
    )
    layer_out[...] = (residual + dot(hidden, w_down[...])).astype(BF16)
    grad_upper = (dot(cotangent[...], w_down[...], NT) * curve).astype(BF16)
    grad_upper_out[...] = grad_upper
    grad_unit = dot(grad_upper, w_up[...], NT) * gain_row
    grad_norm = scale * (
        grad_unit
        - jnp.mean(grad_unit, axis=-1, keepdims=True)
        - unit * jnp.mean(grad_unit * unit, axis=-1, keepdims=True)
    )
    grad_resid = (cotangent[...].astype(F32) + grad_norm).astype(BF16)
    grad_resid_out[...] = grad_resid
    grad_att = dot(grad_resid, w_out[...], NT).astype(BF16)
    grad_att_out[...] = grad_att
    grad_att_t = grad_att.T
    for h in range(heads):
        j = h % per
        canon[h // per, j * width : (j + 1) * width, :] = dot(
            grad_att_t[h * width : (h + 1) * width],
            weights[:, h * slices : (h + 1) * slices].astype(BF16),
        )
    for pos in range(groups):
        value = canon[bit_reverse(pos, bits) ^ mine]
        if pos < groups // 2:
            keep[pos] = value
        else:
            send[pos - groups // 2] = value


def outer_kernel(attended, second, hidden, grad_upper, grad_resid, cotangent, out):
    inner, outer, rows, model = out.shape
    parts = inner * outer
    step = model // parts
    wide = hidden.shape[1] // model
    grad_out = dot(attended[...], grad_resid[...], TN)
    grad_up = dot(second[...], grad_upper[...], TN)
    grad_down = dot(hidden[...], cotangent[...], TN)
    for p in range(parts):
        lo, hi = p % inner, p // inner
        at = slice(p * step, (p + 1) * step)
        out[lo, hi, :step, :] = grad_out[at]
        for w in range(wide):
            out[lo, hi, step * (1 + w) : step * (2 + w), :] = grad_up[
                at, w * model : (w + 1) * model
            ]
        out[lo, hi, step * (1 + wide) :, :] = grad_down[p * step * wide : (p + 1) * step * wide]


def back_kernel(rel, sharpness, *refs):
    groups = len(rel)
    pieces = refs[:groups]
    mixed = refs[groups : 2 * groups]
    (
        weights,
        features,
        middle_t,
        normed,
        grad_att,
        w_slice,
        keep,
        send,
        slice_out,
        grad_mix,
        canon,
        mix_canon,
        mix_map,
        field_map,
        geo_map,
        slice_map,
        logit,
        right,
        total,
    ) = refs[2 * groups :]
    me = lax.axis_index("pts")
    rows, model = grad_att.shape
    width, slices = w_slice.shape
    heads = model // width
    per = heads // groups
    mine = me & (groups - 1)
    base = 2 * per * width
    for r, piece, mix_piece in zip(rel, pieces, mixed):
        canon[mine ^ r] = piece[...]
        mix_canon[mine ^ r] = mix_piece[...]

    def rows_of(ref, offset):
        def of(h):
            row = (offset * per + h % per) * width
            return ref[h // per, row : row + width, :]

        return of

    spread_heads(mix_map, heads, width, slices, rows_of(mix_canon, 0))
    spread_heads(field_map, heads, width, slices, rows_of(canon, 0))
    spread_heads(geo_map, heads, width, slices, rows_of(canon, 1))
    spread_heads(slice_map, heads, width, slices, lambda h: w_slice[...])
    slice_out[...] = jnp.zeros_like(slice_out)

    def block(at, geo):
        numer_map = geo_map if geo else field_map
        feats = features[at, :]
        low = weights[at, :].astype(BF16)
        grad_features = dot(low, numer_map[...], NT)
        right[at, :model] = grad_features.astype(BF16)
        for h in range(heads):
            cols = slice(h * slices, (h + 1) * slices)
            den_row = base + int(geo) * per + h % per
            grad_weights = dot(feats, numer_map[:, cols]) + canon[
                h // per, den_row : den_row + 1, :
            ]
            if not geo:
                grad_weights += dot(grad_att[...], mix_map[:, cols])
            share = weights[at, cols]
            inner = jnp.sum(share * grad_weights, axis=1, keepdims=True)
            low_logit = (share * (grad_weights - inner) * sharpness[h]).astype(BF16)
            logit[:, cols] = low_logit
            slice_out[...] += dot(middle_t[h * width : (h + 1) * width, at], low_logit)
        right[at, model:] = dot(logit[...], slice_map[...], NT).astype(BF16)

    block(pl.ds(0, rows), False)

    @pl.loop(1, normed.shape[0] // rows)
    def _(i):
        block(pl.ds(pl.multiple_of(i * rows, rows), rows), True)

    total[...] = dot(normed[...], right[...], TN)
    half = keep.shape[0]
    step = keep.shape[1] // 2
    bits = (2 * half).bit_length() - 1
    for pos in range(2 * half):
        start = pl.multiple_of((bit_reverse(pos, bits) ^ me) * step, step)
        value = total[pl.ds(start, step), :]
        target = keep if pos < half else send
        target[pos % half, :step, :] = value[:, :model]
        target[pos % half, step:, :] = value[:, model:]

    small_rows = width // 2
    packed = canon[0, canon.shape[1] - small_rows :, :]
    for g in range(1, groups):
        packed += canon[g, canon.shape[1] - small_rows :, :]
    wide = jnp.concatenate([packed[:, : slices // 2], packed[:, slices // 2 :]], axis=0)
    for i in range(3):
        grad_mix[i] = wide[:, i * width : (i + 1) * width]


VMEM = pl.BlockSpec(memory_space=pltpu.VMEM)
SMEM = pl.BlockSpec(memory_space=pltpu.SMEM)


def shape(dims, dtype=F32):
    return jax.ShapeDtypeStruct(tuple(dims), dtype)


def run(body, in_specs, out_shape, scratch, name, *args):
    return pl.pallas_call(
        body,
        out_shape=out_shape,
        in_specs=in_specs,
        out_specs=jax.tree.map(lambda _: VMEM, out_shape),
        scratch_shapes=scratch,
        compiler_params=pltpu.CompilerParams(vmem_limit_bytes=56 * 1024 * 1024),
        name=name,
    )(*args)


def on_device(
    parts,
    points,
    geometry,
    counts,
    cotangent,
    gain_attn,
    w_feat,
    w_mid,
    w_slice,
    sharpness,
    w_query,
    w_key,
    w_value,
    w_out,
    gain_mlp,
    w_up,
    w_down,
):
    rows, model = points.shape
    all_rows = rows + geometry.shape[0]
    width, slices = w_slice.shape
    heads = sharpness.shape[0]
    hidden_width = w_up.shape[1]
    all_bits = parts.bit_length() - 1
    bits = min(GROUP_BITS, all_bits)
    groups = 1 << bits
    per = heads // groups
    token_height = 2 * per * width + pad_to(2 * per, 8)
    grad_height = token_height + width // 2
    half = groups // 2

    def exchange(value, bit):
        return lax.ppermute(value, "pts", [(i, i ^ (1 << bit)) for i in range(parts)])

    def halve(keep, send, first, last):
        for bit in range(first, last):
            got = exchange(send, bit)
            if bit < last - 1:
                count = keep.shape[0] // 2
                keep, send = keep[:count] + got[:count], keep[count:] + got[count:]
            else:
                keep = keep + got
        return keep

    def add_all(value, first, last):
        for bit in range(first, last):
            value = value + exchange(value, bit)
        return value

    def collect(value):
        pieces, rel = [value], [0]
        for bit in reversed(range(bits)):
            pieces = pieces + [exchange(piece, bit) for piece in pieces]
            rel = rel + [r ^ (1 << bit) for r in rel]
        return pieces, tuple(rel)

    keep, send, normed, features, middle_t, weights = run(
        sums_kernel,
        [SMEM, SMEM] + [VMEM] * 6,
        (
            shape((half, token_height, slices)),
            shape((half, token_height, slices)),
            shape((all_rows, model), BF16),
            shape((all_rows, model), BF16),
            shape((model, all_rows), BF16),
            shape((all_rows, heads * slices)),
        ),
        [
            pltpu.VMEM((groups, token_height, slices), F32),
            pltpu.VMEM((model, heads * slices), BF16),
        ],
        "slice_sums",
        counts,
        sharpness,
        points,
        geometry,
        gain_attn,
        w_feat,
        w_mid,
        w_slice,
    )
    tokens = add_all(halve(keep, send, 0, bits)[0], bits, all_bits)
    mixed, attention = run(
        mix_kernel,
        [VMEM] * 4,
        (shape((per * width, slices)), shape((per, 2 * slices, slices))),
        [],
        "mix_tokens",
        tokens,
        w_query,
        w_key,
        w_value,
    )
    mixed_pieces, rel = collect(mixed)
    (
        layer_out,
        grad_att,
        keep,
        send,
        attended,
        second,
        hidden,
        grad_upper,
        grad_resid,
    ) = run(
        functools.partial(mlp_kernel, rel),
        [VMEM] * (groups + 7),
        (
            shape((rows, model), BF16),
            shape((rows, model), BF16),
            shape((half, per * width, slices)),
            shape((half, per * width, slices)),
            shape((rows, model), BF16),
            shape((rows, model), BF16),
            shape((rows, hidden_width), BF16),
            shape((rows, hidden_width), BF16),
            shape((rows, model), BF16),
        ),
        [
            pltpu.VMEM((groups, per * width, slices), F32),
            pltpu.VMEM((model, heads * slices), BF16),
        ],
        "mlp",
        *mixed_pieces,
        weights[:rows],
        points,
        cotangent,
        w_out,
        gain_mlp,
        w_up,
        w_down,
    )
    mixed_grad = add_all(halve(keep, send, 0, bits)[0], bits, all_bits)
    step = model // parts
    wide = hidden_width // model
    outer = run(
        outer_kernel,
        [VMEM] * 6,
        shape((groups, parts // groups, step * (1 + 2 * wide), model)),
        [],
        "weight_grads",
        attended,
        second,
        hidden,
        grad_upper,
        grad_resid,
        cotangent,
    )
    near = [[g * groups + i for i in range(groups)] for g in range(parts // groups)]
    far = [[g * groups + i for g in range(parts // groups)] for i in range(groups)]
    outer = lax.psum_scatter(
        outer, "pts", scatter_dimension=0, axis_index_groups=near, tiled=False
    )
    outer = lax.psum_scatter(outer, "pts", scatter_dimension=0, axis_index_groups=far, tiled=False)
    token_grad = run(
        mix_back_kernel,
        [VMEM] * 6,
        shape((grad_height, slices)),
        [],
        "mix_back",
        tokens,
        attention,
        mixed_grad,
        w_query,
        w_key,
        w_value,
    )
    grad_pieces, rel = collect(token_grad)
    keep, send, slice_sum, grad_mix = run(
        functools.partial(back_kernel, rel),
        [SMEM] + [VMEM] * (2 * groups + 6),
        (
            shape((parts // 2, 2 * step, model)),
            shape((parts // 2, 2 * step, model)),
            shape((width, slices)),
            shape((3, width, width)),
        ),
        [
            pltpu.VMEM((groups, grad_height, slices), F32),
            pltpu.VMEM((groups, per * width, slices), F32),
        ]
        + [pltpu.VMEM((model, heads * slices), BF16)] * 4
        + [
            pltpu.VMEM((rows, heads * slices), BF16),
            pltpu.VMEM((all_rows, 2 * model), BF16),
            pltpu.VMEM((model, 2 * model), F32),
        ],
        "point_back",
        sharpness,
        *grad_pieces,
        *mixed_pieces,
        weights,
        features,
        middle_t,
        normed,
        grad_att,
        w_slice,
    )
    for bit in range(all_bits):
        joined = jnp.concatenate([send.reshape(-1, model), slice_sum], axis=0)
        got = exchange(joined, bit)
        count = keep.shape[0]
        part = got[: count * 2 * step].reshape(keep.shape)
        slice_sum = slice_sum + got[count * 2 * step :]
        if bit < all_bits - 1:
            count //= 2
            keep, send = keep[:count] + part[:count], keep[count:] + part[count:]
        else:
            keep = keep + part
    grad_feat = keep[0, :step]
    grad_mid = keep[0, step:]
    grad_out = outer[:step]
    grad_up = jnp.concatenate(
        [outer[step * (1 + w) : step * (2 + w)] for w in range(wide)], axis=1
    )
    grad_down = outer[step * (1 + wide) :]
    return (layer_out, grad_feat, grad_mid, grad_out, grad_up, grad_down, slice_sum, grad_mix)


def solution(mesh):
    split = P(("design", "pts"), None)
    placed = (split, split, P(("design", "pts")), split) + (P(),) * 12
    return jax.shard_map(
        functools.partial(on_device, mesh.shape["pts"]),
        mesh=mesh,
        in_specs=placed,
        out_specs=(split,) * 6 + (P("design", None), P("design", None, None)),
        check_vma=False,
    )
```

```python
import functools
import math

import jax
import jax.numpy as jnp
from jax import lax
from jax.experimental import pallas as pl
from jax.experimental.pallas import tpu as pltpu
from jax.sharding import PartitionSpec as P

F32 = jnp.float32
BF16 = jnp.bfloat16
EPS = 1e-05
GROUP_BITS = 2
GELU_A = math.sqrt(2.0 / math.pi)
GELU_B = 0.044715

NN = ((1,), (0,))
NT = ((1,), (1,))
TN = ((0,), (0,))


def dot(left, right, dims=NN, precision=None):
    return lax.dot_general(
        left, right, (dims, ((), ())), precision=precision, preferred_element_type=F32
    )


def bit_reverse(value, bits):
    out = 0
    for k in range(bits):
        out = (out << 1) | ((value >> k) & 1)
    return out


def norm_parts(inputs):
    centre = jnp.mean(inputs, axis=-1, keepdims=True)
    shifted = inputs - centre
    spread = jnp.mean(shifted * shifted, axis=-1, keepdims=True)
    return shifted, lax.rsqrt(spread + EPS)


def pad_to(count, unit):
    return -(-count // unit) * unit


def split(value):
    high = value.astype(BF16)
    return high, (value - high.astype(F32)).astype(BF16)


def narrow_dot(left, right):
    left_high, left_low = split(left)
    right_high, right_low = split(right)
    return dot(
        jnp.concatenate([left_high, left_high, left_low], axis=0),
        jnp.concatenate([right_high, right_low, right_high], axis=0),
        TN,
    )


def wide_dot(left, right_parts, dims):
    rows = left.shape[0]
    high, low = split(left)
    right_high, right_low = right_parts
    both = dot(jnp.concatenate([high, low], axis=0), right_high, dims)
    return both[:rows] + both[rows:] + dot(high, right_low, dims)


def place_groups(value_of, keep, send, mine):
    half = keep.shape[0]
    bits = (2 * half).bit_length() - 1
    for pos in range(2 * half):
        target = keep if pos < half else send
        target[pos % half] = value_of(bit_reverse(pos, bits) ^ mine)


def sums_kernel(
    counts_hbm,
    sharpness_hbm,
    points_hbm,
    geometry_hbm,
    gain_hbm,
    w_feat_hbm,
    w_mid_hbm,
    w_slice_hbm,
    keep,
    send,
    normed_out,
    features_out,
    middle_out,
    weights_out,
    geo_weights_out,
    low_out,
    geo_low_out,
    total,
    spread,
    maps,
    logit_map,
    logits,
    counts,
    sharpness,
    points,
    geometry,
    gain,
    w_feat,
    w_mid,
    w_slice,
    sems,
):
    copies = [
        pltpu.make_async_copy(source, target, sems.at[i])
        for i, (source, target) in enumerate(
            (
                (w_slice_hbm, w_slice),
                (w_feat_hbm, w_feat),
                (w_mid_hbm, w_mid),
                (gain_hbm, gain),
                (points_hbm, points),
                (geometry_hbm, geometry),
                (sharpness_hbm, sharpness),
                (counts_hbm, counts),
            )
        )
    ]
    for copy in copies:
        copy.start()
    me = lax.axis_index("pts")
    rows, model = points.shape
    width, slices = w_slice.shape
    heads = model // width
    groups = total.shape[0]
    per = heads // groups
    lanes = spread.shape[2]
    logit_map[...] = jnp.zeros_like(logit_map)
    for copy in copies:
        copy.wait()
    slice_t = w_slice[...].T
    for h in range(heads):
        logit_map[h * slices : (h + 1) * slices, h * width : (h + 1) * width] = slice_t
    maps[:model, :] = w_feat[...].T
    maps[model:, :] = w_mid[...].T
    gain_column = jnp.broadcast_to(gain[...].reshape(1, model), (8, model)).T[:, :1]
    live = lax.broadcasted_iota(jnp.int32, (1, rows), 1) < counts[0]

    def block(inputs, at, out_at, weights_ref, low_ref, geo):
        inputs_t = inputs.T.astype(F32)
        shifted = inputs_t - jnp.mean(inputs_t, axis=0, keepdims=True)
        scale = lax.rsqrt(jnp.mean(shifted * shifted, axis=0, keepdims=True) + EPS)
        normed = (shifted * scale * gain_column).astype(BF16)
        both = dot(maps[...], normed).astype(BF16)
        normed_out[:, at] = normed
        features_out[:, at] = both[:model]
        middle_out[:, at] = both[model:]
        logits[...] = dot(logit_map[...], both[model:])
        for h in range(heads):
            cols = slice(h * slices, (h + 1) * slices)
            factor = sharpness[h] * math.log2(math.e)
            for start in range(0, rows, lanes):
                part = logits[cols, start : start + lanes]
                powers = jnp.exp2((part - jnp.max(part, axis=0, keepdims=True)) * factor)
                inverse = 1.0 / jnp.sum(powers, axis=0, keepdims=True)
                if not geo:
                    inverse = jnp.where(live[:, start : start + lanes], inverse, 0.0)
                weights = powers * inverse
                where = pl.ds(out_at + start, lanes)
                weights_ref[cols, where] = weights
                low_ref[cols, where] = weights.astype(BF16)
                if start == 0 and not geo:
                    spread[0, cols, :] = weights
                else:
                    spread[int(geo), cols, :] += weights

    spread[1] = jnp.zeros_like(spread[1])
    block(points[...], pl.ds(0, rows), 0, weights_out, low_out, False)

    @pl.loop(0, geometry.shape[0] // rows)
    def _(i):
        start = pl.multiple_of(i * rows, rows)
        block(
            geometry[pl.ds(start, rows), :],
            pl.ds(pl.multiple_of(start + rows, rows), rows),
            start,
            geo_weights_out,
            geo_low_out,
            True,
        )

    ones = jnp.ones((16, lanes), BF16)
    for geo, (low_ref, at) in enumerate(
        ((low_out, slice(0, rows)), (geo_low_out, slice(rows, rows + geometry.shape[0])))
    ):
        high = spread[geo].astype(BF16)
        rest = spread[geo] - high.astype(F32)
        middle = rest.astype(BF16)
        low = (rest - middle.astype(F32)).astype(BF16)
        sums = dot(ones, high, NT) + dot(ones, middle, NT) + dot(ones, low, NT)
        for h in range(heads):
            g, j = h // per, h % per
            row = 2 * per * width + geo * per + j
            total[g, row : row + 1, :] = sums[:1, h * slices : (h + 1) * slices]
            row = (geo * per + j) * width
            total[g, row : row + width, :] = dot(
                features_out[h * width : (h + 1) * width, at],
                low_ref[h * slices : (h + 1) * slices, :],
                NT,
            )
    filled = 2 * per * (width + 1)
    total[:, filled:, :] = jnp.zeros((groups, total.shape[1] - filled, slices), F32)
    place_groups(lambda g: total[g], keep, send, me & (groups - 1))


tie = lax.optimization_barrier


def token_rows(tokens, j, per, width):
    base = 2 * per * width
    out = []
    for geo in range(2):
        row = (geo * per + j) * width
        den = tokens[base + geo * per + j : base + geo * per + j + 1, :] + EPS
        out.append((tokens[row : row + width, :] / den, den))
    return out


def mix_kernel(tokens, w_query, w_key, w_value, mixed_out, attention_out, kept):
    width = w_query.shape[0]
    per = attention_out.shape[0]
    slices = tokens.shape[1]
    for j in range(per):
        (field, _), (geo, _) = token_rows(tokens, j, per, width)
        both = jnp.concatenate([field, geo], axis=1)
        query = narrow_dot(w_query[...], field)
        keys = narrow_dot(w_key[...], both)
        values = narrow_dot(w_value[...], both)
        kept[j, :width, :slices] = query
        kept[j, width : 2 * width, :] = keys
        kept[j, 2 * width :, :] = values
        scores = narrow_dot(keys, query)
        scores = (scores - jnp.max(scores, axis=0, keepdims=True)) * (
            math.log2(math.e) / math.sqrt(width)
        )
        powers = jnp.exp2(scores)
        attention = powers * (1.0 / jnp.sum(powers, axis=0, keepdims=True))
        attention_out[j] = attention
        mixed_out[j * width : (j + 1) * width, :] = wide_dot(values, split(attention), NN)


def mix_back_kernel(tokens, attention_in, kept, grad, w_query, w_key, w_value, out):
    width = w_query.shape[0]
    per, both_count, slices = attention_in.shape
    base = 2 * per * width
    small = jnp.zeros((width, 3 * width), F32)
    out[base : base + pad_to(2 * per, 8), :] = jnp.zeros((pad_to(2 * per, 8), slices), F32)
    w_query_t, w_key_t, w_value_t = w_query[...].T, w_key[...].T, w_value[...].T
    for j in range(per):
        (field, field_den), (geo, geo_den) = token_rows(tokens, j, per, width)
        both = jnp.concatenate([field, geo], axis=1)
        query = kept[j, :width, :slices]
        keys = kept[j, width : 2 * width, :]
        values = kept[j, 2 * width :, :]
        attention = attention_in[j]
        mixed_grad = grad[j * width : (j + 1) * width, :]
        att_grad = narrow_dot(values, mixed_grad)
        inner = jnp.sum(attention * att_grad, axis=0, keepdims=True)
        score_grad = split(attention * (att_grad - inner) * (1.0 / math.sqrt(width)))
        value_grad = wide_dot(mixed_grad, split(attention), NT)
        query_grad = wide_dot(keys, score_grad, NN)
        key_grad = wide_dot(query, score_grad, NT)
        both_grad = narrow_dot(w_key_t, key_grad) + narrow_dot(w_value_t, value_grad)
        field_grad = both_grad[:, :slices] + narrow_dot(w_query_t, query_grad)
        geo_grad = both_grad[:, slices:]
        small += jnp.concatenate(
            [
                wide_dot(field, split(query_grad), NT),
                wide_dot(both, split(key_grad), NT),
                wide_dot(both, split(value_grad), NT),
            ],
            axis=1,
        )
        for g, (value, den, value_of) in enumerate(
            ((field_grad, field_den, field), (geo_grad, geo_den, geo))
        ):
            row = (g * per + j) * width
            scaled = value / den
            out[row : row + width, :] = scaled
            out[base + g * per + j : base + g * per + j + 1, :] = -jnp.sum(
                scaled * value_of, axis=0, keepdims=True
            )
    half = width // 2
    filler = jnp.zeros((width, slices // 2 - 3 * width), F32)
    wide = jnp.concatenate([small, filler], axis=1)
    out[out.shape[0] - half :, :] = jnp.concatenate([wide[:half], wide[half:]], axis=1)


def mlp_kernel(
    rel,
    *refs,
):
    groups = len(rel)
    pieces = refs[:groups]
    (
        low,
        points,
        cotangent,
        w_out,
        gain,
        w_up,
        w_down,
        layer_out,
        grad_att_out,
        keep,
        send,
        attended,
        second_out,
        hidden_out,
        grad_upper_out,
        grad_resid_out,
        canon,
    ) = refs[groups:]
    me = lax.axis_index("pts")
    model = points.shape[1]
    slices = canon.shape[2]
    heads = low.shape[0] // slices
    width = model // heads
    per = heads // groups
    mine = me & (groups - 1)
    for r, piece in zip(rel, pieces):
        canon[mine ^ r] = piece[...]
    for h in range(heads):
        cols = slice(h * slices, (h + 1) * slices)
        j = h % per
        attended[h * width : (h + 1) * width, :] = dot(
            canon[h // per, j * width : (j + 1) * width, :].astype(BF16), low[cols, :]
        ).astype(BF16)
    gain_row = gain[...].reshape(1, model)
    residual = points[...].astype(F32) + dot(attended[...], w_out[...], TN)
    shifted, scale = norm_parts(residual)
    unit = shifted * scale
    second = (unit * gain_row).astype(BF16)
    second_out[...] = second
    upper = dot(second, w_up[...])
    square = upper * upper
    slope = jnp.tanh(GELU_A * upper * (1.0 + GELU_B * square))
    half = 0.5 * (1.0 + slope)
    hidden = (upper * half).astype(BF16)
    hidden_out[...] = hidden
    curve = half + 0.5 * upper * (1.0 - slope * slope) * (
        GELU_A * (1.0 + 3.0 * GELU_B * square)
    )
    layer_out[...] = (residual + dot(hidden, w_down[...])).astype(BF16)
    grad_upper = (dot(cotangent[...], w_down[...], NT) * curve).astype(BF16)
    grad_upper_out[...] = grad_upper
    grad_unit = dot(grad_upper, w_up[...], NT) * gain_row
    grad_norm = scale * (
        grad_unit
        - jnp.mean(grad_unit, axis=-1, keepdims=True)
        - unit * jnp.mean(grad_unit * unit, axis=-1, keepdims=True)
    )
    grad_resid = (cotangent[...].astype(F32) + grad_norm).astype(BF16)
    grad_resid_out[...] = grad_resid
    grad_att = dot(w_out[...], grad_resid, NT).astype(BF16)
    grad_att_out[...] = grad_att
    for h in range(heads):
        j = h % per
        canon[h // per, j * width : (j + 1) * width, :] = dot(
            grad_att[h * width : (h + 1) * width], low[h * slices : (h + 1) * slices, :], NT
        )
    place_groups(lambda g: canon[g], keep, send, mine)


def outer_kernel(
    attended, second, hidden, grad_upper, grad_resid, cotangent, keep, send, out, up, down
):
    me = lax.axis_index("pts")
    half, rows, model = keep.shape
    parts = 2 * half
    bits = parts.bit_length() - 1
    step = model // parts
    wide = hidden.shape[1] // model
    out[...] = dot(attended[...], grad_resid[...])
    up[...] = dot(second[...], grad_upper[...], TN)
    down[...] = dot(hidden[...], cotangent[...], TN)
    for pos in range(parts):
        target = keep if pos < half else send
        p = bit_reverse(pos, bits) ^ me
        i = pos % half
        at = pl.ds(pl.multiple_of(p * step, step), step)
        target[i, :step, :] = out[at, :]
        for w in range(wide):
            target[i, step * (1 + w) : step * (2 + w), :] = up[at, w * model : (w + 1) * model]
        tall = step * wide
        target[i, step * (1 + wide) :, :] = down[pl.ds(pl.multiple_of(p * tall, tall), tall), :]


def back_kernel(rel, sharpness, *refs):
    groups = len(rel)
    pieces = refs[:groups]
    mixed = refs[groups : 2 * groups]
    (
        weights,
        geo_weights,
        low,
        geo_low,
        features,
        middle,
        normed,
        grad_att,
        w_slice,
        keep,
        send,
        grad_mix,
        canon,
        mix_canon,
        left_field,
        left_geo,
        low_numer,
        right,
        total,
        slice_sum,
        products,
        logit,
    ) = refs[2 * groups :]
    me = lax.axis_index("pts")
    model, rows = grad_att.shape
    width, slices = w_slice.shape
    heads = model // width
    per = heads // groups
    mine = me & (groups - 1)
    base = 2 * per * width
    for r, piece, mix_piece in zip(rel, pieces, mixed):
        canon[mine ^ r] = piece[...]
        mix_canon[mine ^ r] = mix_piece[...]
    for h in range(heads):
        g, j = h // per, h % per
        for geo in range(2):
            row = (geo * per + j) * width
            numer = canon[g, row : row + width, :].astype(BF16)
            low_numer[geo, h * width : (h + 1) * width, :] = numer
            den = canon[g, base + geo * per + j : base + geo * per + j + 1, :]
            high = den.astype(BF16).astype(F32)
            middle_part = (den - high).astype(BF16).astype(F32)
            rest = den - high - middle_part
            den_rows = jnp.concatenate([high, middle_part, rest, jnp.zeros((13, slices), F32)], axis=0)
            parts = [numer.astype(F32)]
            if not geo:
                parts.append(mix_canon[g, j * width : (j + 1) * width, :])
            parts.append(den_rows)
            left = jnp.concatenate(parts, axis=0).astype(BF16).T
            if geo:
                left_geo[h] = left
            else:
                left_field[h] = left
    slice_sum[...] = jnp.zeros_like(slice_sum)
    ones = jnp.ones((16, rows), BF16)

    def block(at, own_at, weights_ref, low_ref, geo):
        left_ref = left_geo if geo else left_field
        for h in range(heads):
            own = slice(h * width, (h + 1) * width)
            stack = [features[own, at]]
            if not geo:
                stack.append(grad_att[own, :])
            products[h * slices : (h + 1) * slices, :] = dot(
                left_ref[h], jnp.concatenate(stack + [ones], axis=0)
            )
        for h in range(heads):
            cols = slice(h * slices, (h + 1) * slices)
            for start in range(0, rows, lanes):
                grad_weights = products[cols, start : start + lanes]
                share = weights_ref[cols, pl.ds(own_at + start, lanes)]
                inner = jnp.sum(share * grad_weights, axis=0, keepdims=True)
                logit[cols, start : start + lanes] = (
                    share * (grad_weights - inner) * sharpness[h]
                ).astype(BF16)
        for h in range(heads):
            cols = slice(h * slices, (h + 1) * slices)
            own = slice(h * width, (h + 1) * width)
            right[own, at] = dot(
                low_numer[int(geo), own, :], low_ref[cols, pl.ds(own_at, rows)]
            ).astype(BF16)
            right[model + h * width : model + (h + 1) * width, at] = dot(
                w_slice[...], logit[cols, :]
            ).astype(BF16)
            slice_sum[...] += dot(middle[own, at], logit[cols, :], NT)

    lanes = math.gcd(rows, 128)
    block(pl.ds(0, rows), 0, weights, low, False)

    @pl.loop(0, normed.shape[1] // rows - 1)
    def _(i):
        start = pl.multiple_of(i * rows, rows)
        block(pl.ds(pl.multiple_of(start + rows, rows), rows), start, geo_weights, geo_low, True)

    total[...] = dot(normed[...], right[...], NT)
    half = keep.shape[0] // 2
    step = model // (2 * half)
    bits = (2 * half).bit_length() - 1
    for pos in range(2 * half):
        start = pl.multiple_of((bit_reverse(pos, bits) ^ me) * step, step)
        value = total[pl.ds(start, step), :]
        if pos < half:
            keep[2 * pos] = value[:, :model]
            keep[2 * pos + 1] = value[:, model:]
        else:
            row = (pos - half) * 2 * step
            send[row : row + step, :] = value[:, :model]
            send[row + step : row + 2 * step, :] = value[:, model:]
    send[half * 2 * step :, :] = slice_sum[...]

    small_rows = width // 2
    packed = canon[0, canon.shape[1] - small_rows :, :]
    for g in range(1, groups):
        packed += canon[g, canon.shape[1] - small_rows :, :]
    wide = jnp.concatenate([packed[:, : slices // 2], packed[:, slices // 2 :]], axis=0)
    for i in range(3):
        grad_mix[i] = wide[:, i * width : (i + 1) * width]


VMEM = pl.BlockSpec(memory_space=pltpu.VMEM)
SMEM = pl.BlockSpec(memory_space=pltpu.SMEM)
HBM = pl.BlockSpec(memory_space=pltpu.HBM)
MIB = 1024 * 1024


def shape(dims, dtype=F32):
    return jax.ShapeDtypeStruct(tuple(dims), dtype)


def run(body, name, limit, first, out_shape, scratch, *args):
    rest = HBM if first is HBM else VMEM
    if first is HBM:
        args = args[:1] + tuple(
            pltpu.with_memory_space_constraint(arg, pltpu.HBM) for arg in args[1:]
        )
    return pl.pallas_call(
        body,
        out_shape=out_shape,
        in_specs=[first] + [rest] * (len(args) - 1),
        out_specs=jax.tree.map(lambda _: VMEM, out_shape),
        scratch_shapes=scratch,
        compiler_params=pltpu.CompilerParams(vmem_limit_bytes=limit * MIB),
        name=name,
    )(*args)


def on_device(
    parts,
    points,
    geometry,
    counts,
    cotangent,
    gain_attn,
    w_feat,
    w_mid,
    w_slice,
    sharpness,
    w_query,
    w_key,
    w_value,
    w_out,
    gain_mlp,
    w_up,
    w_down,
):
    rows, model = points.shape
    geo_rows = geometry.shape[0]
    all_rows = rows + geo_rows
    width, slices = w_slice.shape
    heads = sharpness.shape[0]
    hidden_width = w_up.shape[1]
    all_bits = parts.bit_length() - 1
    bits = min(GROUP_BITS, all_bits)
    groups = 1 << bits
    per = heads // groups
    token_height = 2 * per * width + pad_to(2 * per, 8)
    grad_height = token_height + width // 2
    half = groups // 2
    step = model // parts
    wide = hidden_width // model

    def exchange(value, bit):
        return lax.ppermute(value, "pts", [(i, i ^ (1 << bit)) for i in range(parts)])

    def fold(keep, got):
        count = keep.shape[0] // 2
        return keep[:count] + got[:count], keep[count:] + got[count:]

    def add_all(value, first, last):
        for bit in range(first, last):
            value = value + exchange(value, bit)
        return value

    def collect(pieces, first, count):
        for bit in reversed(range(first, first + count)):
            pieces = pieces + [exchange(piece, bit) for piece in pieces]
        return pieces

    rel = [0]
    for bit in reversed(range(bits)):
        rel = rel + [r ^ (1 << bit) for r in rel]

    keep, send, normed, features, middle, weights, geo_weights, low, geo_low = run(
        sums_kernel,
        "slice_sums",
        20,
        HBM,
        (
            shape((half, token_height, slices)),
            shape((half, token_height, slices)),
            shape((model, all_rows), BF16),
            shape((model, all_rows), BF16),
            shape((model, all_rows), BF16),
            shape((heads * slices, rows)),
            shape((heads * slices, geo_rows)),
            shape((heads * slices, rows), BF16),
            shape((heads * slices, geo_rows), BF16),
        ),
        [
            pltpu.VMEM((groups, token_height, slices), F32),
            pltpu.VMEM((2, heads * slices, math.gcd(rows, 128)), F32),
            pltpu.VMEM((2 * model, model), BF16),
            pltpu.VMEM((heads * slices, model), BF16),
            pltpu.VMEM((heads * slices, rows), F32),
            pltpu.SMEM(counts.shape, jnp.int32),
            pltpu.SMEM(sharpness.shape, F32),
            pltpu.VMEM(points.shape, BF16),
            pltpu.VMEM(geometry.shape, BF16),
            pltpu.VMEM(gain_attn.shape, F32),
            pltpu.VMEM(w_feat.shape, BF16),
            pltpu.VMEM(w_mid.shape, BF16),
            pltpu.VMEM(w_slice.shape, BF16),
            pltpu.SemaphoreType.DMA((8,)),
        ],
        counts,
        sharpness,
        points,
        geometry,
        gain_attn,
        w_feat,
        w_mid,
        w_slice,
    )
    got = exchange(send, 0)
    for bit in range(1, bits):
        keep, send = fold(keep, got)
        got = exchange(send, bit)
    tokens = add_all((keep + got)[0], bits, all_bits)
    mixed, attention, kept = run(
        mix_kernel,
        "mix_tokens",
        12,
        VMEM,
        (
            shape((per * width, slices)),
            shape((per, 2 * slices, slices)),
            shape((per, 3 * width, 2 * slices)),
        ),
        [],
        tokens,
        w_query,
        w_key,
        w_value,
    )
    mixed_pieces = collect([mixed], 0, bits)
    (
        layer_out,
        grad_att,
        keep,
        send,
        attended,
        second,
        hidden,
        grad_upper,
        grad_resid,
    ) = run(
        functools.partial(mlp_kernel, tuple(rel)),
        "mlp",
        24,
        VMEM,
        (
            shape((rows, model), BF16),
            shape((model, rows), BF16),
            shape((half, per * width, slices)),
            shape((half, per * width, slices)),
            shape((model, rows), BF16),
            shape((rows, model), BF16),
            shape((rows, hidden_width), BF16),
            shape((rows, hidden_width), BF16),
            shape((rows, model), BF16),
        ),
        [pltpu.VMEM((groups, per * width, slices), F32)],
        *mixed_pieces,
        low,
        points,
        cotangent,
        w_out,
        gain_mlp,
        w_up,
        w_down,
    )
    got = exchange(send, 0)
    attended, second, hidden, grad_upper, grad_resid, got = tie(
        (attended, second, hidden, grad_upper, grad_resid, got)
    )
    outer_keep, outer_send = run(
        outer_kernel,
        "weight_grads",
        16,
        VMEM,
        (shape((parts // 2, step * (1 + 2 * wide), model)),) * 2,
        [
            pltpu.VMEM((model, model), F32),
            pltpu.VMEM((model, hidden_width), F32),
            pltpu.VMEM((hidden_width, model), F32),
        ],
        attended,
        second,
        hidden,
        grad_upper,
        grad_resid,
        cotangent,
    )
    for bit in range(1, bits):
        keep, send = fold(keep, got)
        got = exchange(send, bit)
    outer_got = exchange(outer_send, 0)
    mixed_grad, outer_got = tie(((keep + got)[0], outer_got))
    outer_keep, outer_send = fold(outer_keep, outer_got)
    outer_got = exchange(outer_send, 1)
    mixed_grad = add_all(mixed_grad, bits, all_bits)
    token_grad = run(
        mix_back_kernel,
        "mix_back",
        16,
        VMEM,
        shape((grad_height, slices)),
        [],
        tokens,
        attention,
        kept,
        mixed_grad,
        w_query,
        w_key,
        w_value,
    )
    token_grad, outer_got = tie((token_grad, outer_got))
    outer_keep, outer_send = fold(outer_keep, outer_got)
    outer_got = exchange(outer_send, 2)
    grad_pieces = collect([token_grad], 0, bits)
    grad_pieces, outer_got = tie((grad_pieces, outer_got))
    outer_keep, outer_send = fold(outer_keep, outer_got)
    outer_got = exchange(outer_send, 3)
    keep, send, grad_mix = run(
        functools.partial(back_kernel, tuple(rel)),
        "point_back",
        24,
        SMEM,
        (
            shape((parts, step, model)),
            shape((parts * step + width, model)),
            shape((3, width, width)),
        ),
        [
            pltpu.VMEM((groups, grad_height, slices), F32),
            pltpu.VMEM((groups, per * width, slices), F32),
            pltpu.VMEM((heads, slices, 2 * width + 16), BF16),
            pltpu.VMEM((heads, slices, width + 16), BF16),
            pltpu.VMEM((2, model, slices), BF16),
            pltpu.VMEM((2 * model, all_rows), BF16),
            pltpu.VMEM((model, 2 * model), F32),
            pltpu.VMEM((width, slices), F32),
            pltpu.VMEM((heads * slices, rows), F32),
            pltpu.VMEM((heads * slices, rows), BF16),
        ],
        sharpness,
        *grad_pieces,
        *mixed_pieces,
        weights,
        geo_weights,
        low,
        geo_low,
        features,
        middle,
        normed,
        grad_att,
        w_slice,
    )
    keep = keep.reshape(-1, model)
    slice_sum = send[keep.shape[0] :]
    for bit in range(all_bits):
        if bit < all_bits - 3:
            send, outer_got = tie((send, outer_got))
        if bit < all_bits - 4:
            outer_keep, outer_send = fold(outer_keep, outer_got)
            outer_got = exchange(outer_send, bit + 4)
        got = exchange(send, bit)
        count = keep.shape[0]
        slice_sum = slice_sum + got[count:]
        if bit < all_bits - 1:
            count //= 2
            send = jnp.concatenate([keep[count:] + got[count : 2 * count], slice_sum], axis=0)
            keep = keep[:count] + got[:count]
        else:
            grad_feat = keep[:step] + got[:step]
            grad_mid = keep[step:] + got[step : 2 * step]
    outer = (outer_keep + outer_got)[0]
    grad_out = outer[:step]
    grad_up = jnp.concatenate(
        [outer[step * (1 + w) : step * (2 + w)] for w in range(wide)], axis=1
    )
    grad_down = outer[step * (1 + wide) :]
    return (layer_out, grad_feat, grad_mid, grad_out, grad_up, grad_down, slice_sum, grad_mix)


def solution(mesh):
    split = P(("design", "pts"), None)
    placed = (split, split, P(("design", "pts")), split) + (P(),) * 12
    return jax.shard_map(
        functools.partial(on_device, mesh.shape["pts"]),
        mesh=mesh,
        in_specs=placed,
        out_specs=(split,) * 6 + (P("design", None), P("design", None, None)),
        check_vma=False,
    )
```

```python
import functools
import math

import jax
import jax.numpy as jnp
from jax import lax
from jax.experimental import pallas as pl
from jax.experimental.pallas import tpu as pltpu
from jax.sharding import PartitionSpec as P

F32 = jnp.float32
BF16 = jnp.bfloat16
EPS = 1e-05
GROUP_BITS = 2
GELU_A = math.sqrt(2.0 / math.pi)
GELU_B = 0.044715

NN = ((1,), (0,))
NT = ((1,), (1,))
TN = ((0,), (0,))


def dot(left, right, dims=NN, precision=None):
    return lax.dot_general(
        left, right, (dims, ((), ())), precision=precision, preferred_element_type=F32
    )


def bit_reverse(value, bits):
    out = 0
    for k in range(bits):
        out = (out << 1) | ((value >> k) & 1)
    return out


def norm_parts(inputs):
    centre = jnp.mean(inputs, axis=-1, keepdims=True)
    shifted = inputs - centre
    spread = jnp.mean(shifted * shifted, axis=-1, keepdims=True)
    return shifted, lax.rsqrt(spread + EPS)


def pad_to(count, unit):
    return -(-count // unit) * unit


def split(value):
    high = value.astype(BF16)
    return high, (value - high.astype(F32)).astype(BF16)


def narrow_dot(left, right):
    left_high, left_low = split(left)
    right_high, right_low = split(right)
    return dot(
        jnp.concatenate([left_high, left_high, left_low], axis=0),
        jnp.concatenate([right_high, right_low, right_high], axis=0),
        TN,
    )


def wide_dot(left, right_parts, dims):
    rows = left.shape[0]
    high, low = split(left)
    right_high, right_low = right_parts
    both = dot(jnp.concatenate([high, low], axis=0), right_high, dims)
    return both[:rows] + both[rows:] + dot(high, right_low, dims)


def place_groups(value_of, keep, send, mine):
    half = keep.shape[0]
    bits = (2 * half).bit_length() - 1
    for pos in range(2 * half):
        target = keep if pos < half else send
        target[pos % half] = value_of(bit_reverse(pos, bits) ^ mine)


def sums_kernel(
    counts_hbm,
    sharpness_hbm,
    points_hbm,
    geometry_hbm,
    gain_hbm,
    w_feat_hbm,
    w_mid_hbm,
    w_slice_hbm,
    keep,
    send,
    normed_out,
    features_out,
    middle_out,
    weights_out,
    geo_weights_out,
    low_out,
    geo_low_out,
    total,
    maps,
    counts,
    sharpness,
    points,
    geometry,
    gain,
    w_feat,
    w_mid,
    w_slice,
    sems,
):
    copies = [
        pltpu.make_async_copy(source, target, sems.at[i])
        for i, (source, target) in enumerate(
            (
                (w_slice_hbm, w_slice),
                (w_feat_hbm, w_feat),
                (w_mid_hbm, w_mid),
                (gain_hbm, gain),
                (points_hbm, points),
                (geometry_hbm, geometry),
                (sharpness_hbm, sharpness),
                (counts_hbm, counts),
            )
        )
    ]
    for copy in copies:
        copy.start()
    me = lax.axis_index("pts")
    rows, model = points.shape
    all_rows = rows + geometry.shape[0]
    width, slices = w_slice.shape
    heads = model // width
    groups = total.shape[0]
    per = heads // groups
    lanes = math.gcd(rows, 128)
    filled = 2 * per * (width + 1)
    total[:, filled:, :] = jnp.zeros((groups, total.shape[1] - filled, slices), F32)
    for copy in copies[:4]:
        copy.wait()
    slice_t = w_slice[...].T
    maps[:model, :] = w_feat[...].T
    maps[model:, :] = w_mid[...].T
    gain_column = jnp.broadcast_to(gain[...].reshape(1, model), (8, model)).T[:, :1]
    for copy in copies[4:]:
        copy.wait()
    live = lax.broadcasted_iota(jnp.int32, (1, rows), 1) < counts[0]
    blocks = range(0, all_rows, rows)
    for start in blocks:
        at = slice(start, start + rows)
        inputs = points[...] if start == 0 else geometry[start - rows : start, :]
        inputs_t = inputs.T.astype(F32)
        shifted = inputs_t - jnp.mean(inputs_t, axis=0, keepdims=True)
        scale = lax.rsqrt(jnp.mean(shifted * shifted, axis=0, keepdims=True) + EPS)
        normed = (shifted * scale * gain_column).astype(BF16)
        both = dot(maps[...], normed).astype(BF16)
        normed_out[:, at] = normed
        features_out[:, at] = both[:model]
        middle_out[:, at] = both[model:]

    def logits_of(h):
        own = slice(h * width, (h + 1) * width)
        return [dot(slice_t, middle_out[own, start : start + rows]) for start in blocks]

    def numerators(h):
        own = slice(h * width, (h + 1) * width)
        cols = slice(h * slices, (h + 1) * slices)
        g, j = h // per, h % per
        for geo, (low_ref, at) in enumerate(
            ((low_out, slice(0, rows)), (geo_low_out, slice(rows, all_rows)))
        ):
            row = (geo * per + j) * width
            total[g, row : row + width, :] = dot(features_out[own, at], low_ref[cols, :], NT)

    ahead = logits_of(0)
    for h in range(heads):
        cols = slice(h * slices, (h + 1) * slices)
        logits = ahead
        if h + 1 < heads:
            ahead = logits_of(h + 1)
        factor = sharpness[h] * math.log2(math.e)
        for geo, first in ((0, 0), (1, 1)):
            weights_ref, low_ref = ((weights_out, low_out), (geo_weights_out, geo_low_out))[geo]
            folded = None
            for i in range(first, 1 if geo == 0 else len(logits)):
                for start in range(0, rows, lanes):
                    part = logits[i][:, start : start + lanes]
                    powers = jnp.exp2((part - jnp.max(part, axis=0, keepdims=True)) * factor)
                    inverse = 1.0 / jnp.sum(powers, axis=0, keepdims=True)
                    if geo == 0:
                        inverse = jnp.where(live[:, start : start + lanes], inverse, 0.0)
                    weights = powers * inverse
                    where = (i - first) * rows + start
                    weights_ref[cols, where : where + lanes] = weights
                    low_ref[cols, where : where + lanes] = weights.astype(BF16)
                    folded = weights if folded is None else folded + weights
            row = 2 * per * width + geo * per + h % per
            total[h // per, row : row + 1, :] = jnp.sum(folded.T, axis=0, keepdims=True)
        if h > 0:
            numerators(h - 1)
    numerators(heads - 1)

    place_groups(lambda g: total[g], keep, send, me & (groups - 1))


tie = lax.optimization_barrier


def token_rows(tokens, j, per, width):
    base = 2 * per * width
    out = []
    for geo in range(2):
        row = (geo * per + j) * width
        den = tokens[base + geo * per + j : base + geo * per + j + 1, :] + EPS
        out.append((tokens[row : row + width, :] / den, den))
    return out


def mix_kernel(tokens, w_query, w_key, w_value, mixed_out, attention_out, kept):
    width = w_query.shape[0]
    per = attention_out.shape[0]
    slices = tokens.shape[1]
    maps = jnp.concatenate([w_query[...], w_key[...], w_value[...]], axis=1)
    for j in range(per):
        (field, _), (geo, _) = token_rows(tokens, j, per, width)
        both = jnp.concatenate([field, geo], axis=1)
        projected = narrow_dot(maps, both)
        kept[j] = projected
        query = projected[:width, :slices]
        keys = projected[width : 2 * width]
        values = projected[2 * width :]
        scores = narrow_dot(keys, query)
        scores = (scores - jnp.max(scores, axis=0, keepdims=True)) * (
            math.log2(math.e) / math.sqrt(width)
        )
        powers = jnp.exp2(scores)
        attention = powers * (1.0 / jnp.sum(powers, axis=0, keepdims=True))
        attention_out[j] = attention
        mixed_out[j * width : (j + 1) * width, :] = wide_dot(values, split(attention), NN)


def mix_back_kernel(tokens, attention_in, kept, grad, w_query, w_key, w_value, out):
    width = w_query.shape[0]
    per, both_count, slices = attention_in.shape
    base = 2 * per * width
    small = jnp.zeros((width, 3 * width), F32)
    out[base : base + pad_to(2 * per, 8), :] = jnp.zeros((pad_to(2 * per, 8), slices), F32)
    maps_t = jnp.concatenate([w_query[...].T, w_key[...].T, w_value[...].T], axis=0)
    none = jnp.zeros((width, both_count - slices), F32)
    for j in range(per):
        (field, field_den), (geo, geo_den) = token_rows(tokens, j, per, width)
        both = jnp.concatenate([field, geo], axis=1)
        query = kept[j, :width, :slices]
        keys = kept[j, width : 2 * width, :]
        values = kept[j, 2 * width :, :]
        attention = attention_in[j]
        mixed_grad = grad[j * width : (j + 1) * width, :]
        att_grad = narrow_dot(values, mixed_grad)
        inner = jnp.sum(attention * att_grad, axis=0, keepdims=True)
        score_grad = split(attention * (att_grad - inner) * (1.0 / math.sqrt(width)))
        value_grad = wide_dot(mixed_grad, split(attention), NT)
        query_grad = wide_dot(keys, score_grad, NN)
        key_grad = wide_dot(query, score_grad, NT)
        grads = jnp.concatenate(
            [jnp.concatenate([query_grad, none], axis=1), key_grad, value_grad], axis=0
        )
        both_grad = narrow_dot(maps_t, grads)
        field_grad = both_grad[:, :slices]
        geo_grad = both_grad[:, slices:]
        small += wide_dot(both, split(grads), NT)
        for g, (value, den, value_of) in enumerate(
            ((field_grad, field_den, field), (geo_grad, geo_den, geo))
        ):
            row = (g * per + j) * width
            scaled = value / den
            out[row : row + width, :] = scaled
            out[base + g * per + j : base + g * per + j + 1, :] = -jnp.sum(
                scaled * value_of, axis=0, keepdims=True
            )
    half = width // 2
    filler = jnp.zeros((width, slices // 2 - 3 * width), F32)
    wide = jnp.concatenate([small, filler], axis=1)
    out[out.shape[0] - half :, :] = jnp.concatenate([wide[:half], wide[half:]], axis=1)


def mlp_kernel(
    rel,
    *refs,
):
    groups = len(rel)
    pieces = refs[:groups]
    (
        low,
        points,
        cotangent,
        w_out,
        gain,
        w_up,
        w_down,
        layer_out,
        grad_att_out,
        keep,
        send,
        attended,
        second_out,
        hidden_out,
        grad_upper_out,
        grad_resid_out,
        canon,
    ) = refs[groups:]
    me = lax.axis_index("pts")
    model = points.shape[1]
    slices = canon.shape[2]
    heads = low.shape[0] // slices
    width = model // heads
    per = heads // groups
    mine = me & (groups - 1)
    for r, piece in zip(rel, pieces):
        canon[mine ^ r] = piece[...]
    for h in range(heads):
        cols = slice(h * slices, (h + 1) * slices)
        j = h % per
        attended[h * width : (h + 1) * width, :] = dot(
            canon[h // per, j * width : (j + 1) * width, :].astype(BF16), low[cols, :]
        ).astype(BF16)
    gain_row = gain[...].reshape(1, model)
    residual = points[...].astype(F32) + dot(attended[...], w_out[...], TN)
    shifted, scale = norm_parts(residual)
    unit = shifted * scale
    second = (unit * gain_row).astype(BF16)
    second_out[...] = second
    upper = dot(second, w_up[...])
    square = upper * upper
    slope = jnp.tanh(GELU_A * upper * (1.0 + GELU_B * square))
    half = 0.5 * (1.0 + slope)
    hidden = (upper * half).astype(BF16)
    hidden_out[...] = hidden
    curve = half + 0.5 * upper * (1.0 - slope * slope) * (
        GELU_A * (1.0 + 3.0 * GELU_B * square)
    )
    layer_out[...] = (residual + dot(hidden, w_down[...])).astype(BF16)
    grad_upper = (dot(cotangent[...], w_down[...], NT) * curve).astype(BF16)
    grad_upper_out[...] = grad_upper
    grad_unit = dot(grad_upper, w_up[...], NT) * gain_row
    grad_norm = scale * (
        grad_unit
        - jnp.mean(grad_unit, axis=-1, keepdims=True)
        - unit * jnp.mean(grad_unit * unit, axis=-1, keepdims=True)
    )
    grad_resid = (cotangent[...].astype(F32) + grad_norm).astype(BF16)
    grad_resid_out[...] = grad_resid
    grad_att = dot(w_out[...], grad_resid, NT).astype(BF16)
    grad_att_out[...] = grad_att
    for h in range(heads):
        j = h % per
        canon[h // per, j * width : (j + 1) * width, :] = dot(
            grad_att[h * width : (h + 1) * width], low[h * slices : (h + 1) * slices, :], NT
        )
    place_groups(lambda g: canon[g], keep, send, mine)


def outer_kernel(
    attended, second, hidden, grad_upper, grad_resid, cotangent, keep, send, out, up, down
):
    me = lax.axis_index("pts")
    half, rows, model = keep.shape
    parts = 2 * half
    bits = parts.bit_length() - 1
    step = model // parts
    wide = hidden.shape[1] // model
    out[...] = dot(attended[...], grad_resid[...])
    up[...] = dot(second[...], grad_upper[...], TN)
    down[...] = dot(hidden[...], cotangent[...], TN)
    for pos in range(parts):
        target = keep if pos < half else send
        p = bit_reverse(pos, bits) ^ me
        i = pos % half
        at = pl.ds(pl.multiple_of(p * step, step), step)
        target[i, :step, :] = out[at, :]
        for w in range(wide):
            target[i, step * (1 + w) : step * (2 + w), :] = up[at, w * model : (w + 1) * model]
        tall = step * wide
        target[i, step * (1 + wide) :, :] = down[pl.ds(pl.multiple_of(p * tall, tall), tall), :]


def back_kernel(rel, sharpness, *refs):
    groups = len(rel)
    pieces = refs[:groups]
    mixed = refs[groups : 2 * groups]
    (
        weights,
        geo_weights,
        low,
        geo_low,
        features,
        middle,
        normed,
        grad_att,
        w_slice,
        keep,
        send,
        grad_mix,
        canon,
        mix_canon,
        left_field,
        left_geo,
        low_numer,
        right,
        total,
        slice_sum,
        logit,
    ) = refs[2 * groups :]
    me = lax.axis_index("pts")
    model, rows = grad_att.shape
    width, slices = w_slice.shape
    heads = model // width
    per = heads // groups
    mine = me & (groups - 1)
    base = 2 * per * width
    for r, piece, mix_piece in zip(rel, pieces, mixed):
        canon[mine ^ r] = piece[...]
        mix_canon[mine ^ r] = mix_piece[...]
    for h in range(heads):
        g, j = h // per, h % per
        for geo in range(2):
            row = (geo * per + j) * width
            numer = canon[g, row : row + width, :].astype(BF16)
            low_numer[geo, h * width : (h + 1) * width, :] = numer
            den = canon[g, base + geo * per + j : base + geo * per + j + 1, :]
            high = den.astype(BF16).astype(F32)
            middle_part = (den - high).astype(BF16).astype(F32)
            rest = den - high - middle_part
            den_rows = jnp.concatenate([high, middle_part, rest, jnp.zeros((13, slices), F32)], axis=0)
            parts = [numer.astype(F32)]
            if not geo:
                parts.append(mix_canon[g, j * width : (j + 1) * width, :])
            parts.append(den_rows)
            left = jnp.concatenate(parts, axis=0).astype(BF16).T
            if geo:
                left_geo[h] = left
            else:
                left_field[h] = left
    all_rows = normed.shape[1]
    lanes = math.gcd(rows, 128)
    ones = jnp.ones((16, rows), BF16)
    blocks = range(0, all_rows, rows)

    def products_of(h):
        own = slice(h * width, (h + 1) * width)
        out = []
        for start in blocks:
            stack = [features[own, start : start + rows]]
            if start == 0:
                stack.append(grad_att[own, :])
            left = left_field if start == 0 else left_geo
            out.append(dot(left[h], jnp.concatenate(stack + [ones], axis=0)))
        return out

    def finish(h):
        cols = slice(h * slices, (h + 1) * slices)
        own = slice(h * width, (h + 1) * width)
        right[own, :rows] = dot(low_numer[0, own, :], low[cols, :]).astype(BF16)
        right[own, rows:] = dot(low_numer[1, own, :], geo_low[cols, :]).astype(BF16)
        right[model + h * width : model + (h + 1) * width, :] = dot(
            w_slice[...], logit[cols, :]
        ).astype(BF16)
        term = dot(logit[cols, :], middle[own, :], NT)
        if h == 0:
            slice_sum[...] = term
        else:
            slice_sum[...] += term

    ahead = products_of(0)
    for h in range(heads):
        cols = slice(h * slices, (h + 1) * slices)
        products = ahead
        if h + 1 < heads:
            ahead = products_of(h + 1)
        for i, begin in enumerate(blocks):
            for start in range(0, rows, lanes):
                grad_weights = products[i][:, start : start + lanes]
                if i == 0:
                    share = weights[cols, start : start + lanes]
                else:
                    where = begin - rows + start
                    share = geo_weights[cols, where : where + lanes]
                inner = jnp.sum(share * grad_weights, axis=0, keepdims=True)
                logit[cols, begin + start : begin + start + lanes] = (
                    share * (grad_weights - inner) * sharpness[h]
                ).astype(BF16)
        if h > 0:
            finish(h - 1)
    finish(heads - 1)

    total[...] = dot(normed[...], right[...], NT)
    half = keep.shape[0] // 2
    step = model // (2 * half)
    bits = (2 * half).bit_length() - 1
    for pos in range(2 * half):
        start = pl.multiple_of((bit_reverse(pos, bits) ^ me) * step, step)
        value = total[pl.ds(start, step), :]
        if pos < half:
            keep[2 * pos] = value[:, :model]
            keep[2 * pos + 1] = value[:, model:]
        else:
            row = (pos - half) * 2 * step
            send[row : row + step, :] = value[:, :model]
            send[row + step : row + 2 * step, :] = value[:, model:]
    send[half * 2 * step :, :] = slice_sum[...].T

    small_rows = width // 2
    packed = canon[0, canon.shape[1] - small_rows :, :]
    for g in range(1, groups):
        packed += canon[g, canon.shape[1] - small_rows :, :]
    wide = jnp.concatenate([packed[:, : slices // 2], packed[:, slices // 2 :]], axis=0)
    for i in range(3):
        grad_mix[i] = wide[:, i * width : (i + 1) * width]


def finish_kernel(keep, got, slice_sum, feat, mid, slice_out):
    step = feat.shape[0]
    feat[...] = keep[:step, :] + got[:step, :]
    mid[...] = keep[step:, :] + got[step : 2 * step, :]
    slice_out[...] = slice_sum[...] + got[2 * step :, :]


VMEM = pl.BlockSpec(memory_space=pltpu.VMEM)
SMEM = pl.BlockSpec(memory_space=pltpu.SMEM)
HBM = pl.BlockSpec(memory_space=pltpu.HBM)
MIB = 1024 * 1024


def shape(dims, dtype=F32):
    return jax.ShapeDtypeStruct(tuple(dims), dtype)


def run(body, name, limit, first, out_shape, scratch, *args):
    rest = HBM if first is HBM else VMEM
    if first is HBM:
        args = args[:1] + tuple(
            pltpu.with_memory_space_constraint(arg, pltpu.HBM) for arg in args[1:]
        )
    return pl.pallas_call(
        body,
        out_shape=out_shape,
        in_specs=[first] + [rest] * (len(args) - 1),
        out_specs=jax.tree.map(lambda _: VMEM, out_shape),
        scratch_shapes=scratch,
        compiler_params=pltpu.CompilerParams(vmem_limit_bytes=limit * MIB),
        name=name,
    )(*args)


def on_device(
    parts,
    points,
    geometry,
    counts,
    cotangent,
    gain_attn,
    w_feat,
    w_mid,
    w_slice,
    sharpness,
    w_query,
    w_key,
    w_value,
    w_out,
    gain_mlp,
    w_up,
    w_down,
):
    rows, model = points.shape
    geo_rows = geometry.shape[0]
    all_rows = rows + geo_rows
    width, slices = w_slice.shape
    heads = sharpness.shape[0]
    hidden_width = w_up.shape[1]
    all_bits = parts.bit_length() - 1
    bits = min(GROUP_BITS, all_bits)
    groups = 1 << bits
    per = heads // groups
    token_height = 2 * per * width + pad_to(2 * per, 8)
    grad_height = token_height + width // 2
    half = groups // 2
    step = model // parts
    wide = hidden_width // model

    def exchange(value, bit):
        return lax.ppermute(value, "pts", [(i, i ^ (1 << bit)) for i in range(parts)])

    def fold(keep, got):
        count = keep.shape[0] // 2
        return keep[:count] + got[:count], keep[count:] + got[count:]

    def add_all(value, first, last):
        for bit in range(first, last):
            value = value + exchange(value, bit)
        return value

    def collect(pieces, first, count):
        for bit in reversed(range(first, first + count)):
            pieces = pieces + [exchange(piece, bit) for piece in pieces]
        return pieces

    rel = [0]
    for bit in reversed(range(bits)):
        rel = rel + [r ^ (1 << bit) for r in rel]

    keep, send, normed, features, middle, weights, geo_weights, low, geo_low = run(
        sums_kernel,
        "slice_sums",
        20,
        HBM,
        (
            shape((half, token_height, slices)),
            shape((half, token_height, slices)),
            shape((model, all_rows), BF16),
            shape((model, all_rows), BF16),
            shape((model, all_rows), BF16),
            shape((heads * slices, rows)),
            shape((heads * slices, geo_rows)),
            shape((heads * slices, rows), BF16),
            shape((heads * slices, geo_rows), BF16),
        ),
        [
            pltpu.VMEM((groups, token_height, slices), F32),
            pltpu.VMEM((2 * model, model), BF16),
            pltpu.SMEM(counts.shape, jnp.int32),
            pltpu.SMEM(sharpness.shape, F32),
            pltpu.VMEM(points.shape, BF16),
            pltpu.VMEM(geometry.shape, BF16),
            pltpu.VMEM(gain_attn.shape, F32),
            pltpu.VMEM(w_feat.shape, BF16),
            pltpu.VMEM(w_mid.shape, BF16),
            pltpu.VMEM(w_slice.shape, BF16),
            pltpu.SemaphoreType.DMA((8,)),
        ],
        counts,
        sharpness,
        points,
        geometry,
        gain_attn,
        w_feat,
        w_mid,
        w_slice,
    )
    got = exchange(send, 0)
    for bit in range(1, bits):
        keep, send = fold(keep, got)
        got = exchange(send, bit)
    tokens = add_all((keep + got)[0], bits, all_bits)
    mixed, attention, kept = run(
        mix_kernel,
        "mix_tokens",
        12,
        VMEM,
        (
            shape((per * width, slices)),
            shape((per, 2 * slices, slices)),
            shape((per, 3 * width, 2 * slices)),
        ),
        [],
        tokens,
        w_query,
        w_key,
        w_value,
    )
    mixed_pieces = collect([mixed], 0, bits)
    (
        layer_out,
        grad_att,
        keep,
        send,
        attended,
        second,
        hidden,
        grad_upper,
        grad_resid,
    ) = run(
        functools.partial(mlp_kernel, tuple(rel)),
        "mlp",
        24,
        VMEM,
        (
            shape((rows, model), BF16),
            shape((model, rows), BF16),
            shape((half, per * width, slices)),
            shape((half, per * width, slices)),
            shape((model, rows), BF16),
            shape((rows, model), BF16),
            shape((rows, hidden_width), BF16),
            shape((rows, hidden_width), BF16),
            shape((rows, model), BF16),
        ),
        [pltpu.VMEM((groups, per * width, slices), F32)],
        *mixed_pieces,
        low,
        points,
        cotangent,
        w_out,
        gain_mlp,
        w_up,
        w_down,
    )
    got = exchange(send, 0)
    attended, second, hidden, grad_upper, grad_resid, got = tie(
        (attended, second, hidden, grad_upper, grad_resid, got)
    )
    outer_keep, outer_send = run(
        outer_kernel,
        "weight_grads",
        16,
        VMEM,
        (shape((parts // 2, step * (1 + 2 * wide), model)),) * 2,
        [
            pltpu.VMEM((model, model), F32),
            pltpu.VMEM((model, hidden_width), F32),
            pltpu.VMEM((hidden_width, model), F32),
        ],
        attended,
        second,
        hidden,
        grad_upper,
        grad_resid,
        cotangent,
    )
    for bit in range(1, bits):
        keep, send = fold(keep, got)
        got = exchange(send, bit)
    outer_got = exchange(outer_send, 0)
    mixed_grad, outer_got = tie(((keep + got)[0], outer_got))
    outer_keep, outer_send = fold(outer_keep, outer_got)
    outer_got = exchange(outer_send, 1)
    mixed_grad = add_all(mixed_grad, bits, all_bits)
    token_grad = run(
        mix_back_kernel,
        "mix_back",
        16,
        VMEM,
        shape((grad_height, slices)),
        [],
        tokens,
        attention,
        kept,
        mixed_grad,
        w_query,
        w_key,
        w_value,
    )
    token_grad, outer_got = tie((token_grad, outer_got))
    outer_keep, outer_send = fold(outer_keep, outer_got)
    outer_got = exchange(outer_send, 2)
    grad_pieces = collect([token_grad], 0, bits)
    grad_pieces, outer_got = tie((grad_pieces, outer_got))
    outer_keep, outer_send = fold(outer_keep, outer_got)
    outer_got = exchange(outer_send, 3)
    keep, send, grad_mix = run(
        functools.partial(back_kernel, tuple(rel)),
        "point_back",
        24,
        SMEM,
        (
            shape((parts, step, model)),
            shape((parts * step + width, model)),
            shape((3, width, width)),
        ),
        [
            pltpu.VMEM((groups, grad_height, slices), F32),
            pltpu.VMEM((groups, per * width, slices), F32),
            pltpu.VMEM((heads, slices, 2 * width + 16), BF16),
            pltpu.VMEM((heads, slices, width + 16), BF16),
            pltpu.VMEM((2, model, slices), BF16),
            pltpu.VMEM((2 * model, all_rows), BF16),
            pltpu.VMEM((model, 2 * model), F32),
            pltpu.VMEM((slices, width), F32),
            pltpu.VMEM((heads * slices, all_rows), BF16),
        ],
        sharpness,
        *grad_pieces,
        *mixed_pieces,
        weights,
        geo_weights,
        low,
        geo_low,
        features,
        middle,
        normed,
        grad_att,
        w_slice,
    )
    keep = keep.reshape(-1, model)
    slice_sum = send[keep.shape[0] :]
    for bit in range(all_bits):
        if bit < all_bits - 3:
            send, outer_got = tie((send, outer_got))
        if bit < all_bits - 4:
            outer_keep, outer_send = fold(outer_keep, outer_got)
            outer_got = exchange(outer_send, bit + 4)
        got = exchange(send, bit)
        if bit == all_bits - 1:
            break
        slice_sum = slice_sum + got[keep.shape[0] :]
        count = keep.shape[0] // 2
        send = jnp.concatenate([keep[count:] + got[count : 2 * count], slice_sum], axis=0)
        keep = keep[:count] + got[:count]
    grad_feat, grad_mid, grad_slice = run(
        finish_kernel,
        "finish",
        4,
        VMEM,
        (shape((step, model)), shape((step, model)), shape((width, slices))),
        [],
        keep,
        got,
        slice_sum,
    )
    outer = (outer_keep + outer_got)[0]
    grad_out = outer[:step]
    grad_up = jnp.concatenate(
        [outer[step * (1 + w) : step * (2 + w)] for w in range(wide)], axis=1
    )
    grad_down = outer[step * (1 + wide) :]
    return (layer_out, grad_feat, grad_mid, grad_out, grad_up, grad_down, grad_slice, grad_mix)


def solution(mesh):
    split = P(("design", "pts"), None)
    placed = (split, split, P(("design", "pts")), split) + (P(),) * 12
    return jax.shard_map(
        functools.partial(on_device, mesh.shape["pts"]),
        mesh=mesh,
        in_specs=placed,
        out_specs=(split,) * 6 + (P("design", None), P("design", None, None)),
        check_vma=False,
    )
```

```python
import functools
import math

import jax
import jax.numpy as jnp
from jax import lax
from jax.experimental import pallas as pl
from jax.experimental.pallas import tpu as pltpu
from jax.sharding import PartitionSpec as P

F32 = jnp.float32
BF16 = jnp.bfloat16
EPS = 1e-05
GROUP_BITS = 2
GELU_A = math.sqrt(2.0 / math.pi)
GELU_B = 0.044715

NN = ((1,), (0,))
NT = ((1,), (1,))
TN = ((0,), (0,))


def dot(left, right, dims=NN, precision=None):
    return lax.dot_general(
        left, right, (dims, ((), ())), precision=precision, preferred_element_type=F32
    )


def bit_reverse(value, bits):
    out = 0
    for k in range(bits):
        out = (out << 1) | ((value >> k) & 1)
    return out


def from_position(pos, order):
    out = 0
    for i, bit in enumerate(order):
        out |= ((pos >> (len(order) - 1 - i)) & 1) << bit
    return out


def norm_parts(inputs):
    centre = jnp.mean(inputs, axis=-1, keepdims=True)
    shifted = inputs - centre
    spread = jnp.mean(shifted * shifted, axis=-1, keepdims=True)
    return shifted, lax.rsqrt(spread + EPS)


def pad_to(count, unit):
    return -(-count // unit) * unit


def split(value):
    high = value.astype(BF16)
    return high, (value - high.astype(F32)).astype(BF16)


def narrow_dot(left, right):
    left_high, left_low = split(left)
    right_high, right_low = split(right)
    return dot(
        jnp.concatenate([left_high, left_high, left_low], axis=0),
        jnp.concatenate([right_high, right_low, right_high], axis=0),
        TN,
    )


def wide_dot(left, right_parts, dims):
    rows = left.shape[0]
    high, low = split(left)
    right_high, right_low = right_parts
    both = dot(jnp.concatenate([high, low], axis=0), right_high, dims)
    return both[:rows] + both[rows:] + dot(high, right_low, dims)


def place_groups(value_of, keep, send, mine):
    half = keep.shape[0]
    bits = (2 * half).bit_length() - 1
    for pos in range(2 * half):
        target = keep if pos < half else send
        target[pos % half] = value_of(bit_reverse(pos, bits) ^ mine)


def sums_kernel(
    counts_hbm,
    sharpness_hbm,
    points_hbm,
    geometry_hbm,
    gain_hbm,
    w_feat_hbm,
    w_mid_hbm,
    w_slice_hbm,
    keep,
    send,
    normed_out,
    features_out,
    middle_out,
    weights_out,
    geo_weights_out,
    low_out,
    geo_low_out,
    total,
    maps,
    counts,
    sharpness,
    points,
    geometry,
    gain,
    w_feat,
    w_mid,
    w_slice,
    sems,
):
    copies = [
        pltpu.make_async_copy(source, target, sems.at[i])
        for i, (source, target) in enumerate(
            (
                (points_hbm, points),
                (geometry_hbm, geometry),
                (w_feat_hbm, w_feat),
                (w_mid_hbm, w_mid),
                (gain_hbm, gain),
                (w_slice_hbm, w_slice),
                (sharpness_hbm, sharpness),
                (counts_hbm, counts),
            )
        )
    ]
    for copy in copies:
        copy.start()
    me = lax.axis_index("pts")
    rows, model = points.shape
    all_rows = rows + geometry.shape[0]
    width, slices = w_slice.shape
    heads = model // width
    groups = total.shape[0]
    per = heads // groups
    lanes = math.gcd(rows, 128)
    filled = 2 * per * (width + 1)
    total[:, filled:, :] = jnp.zeros((groups, total.shape[1] - filled, slices), F32)
    for copy in copies:
        copy.wait()
    slice_t = w_slice[...].T
    maps[:model, :] = w_feat[...].T
    maps[model:, :] = w_mid[...].T
    gain_column = jnp.broadcast_to(gain[...].reshape(1, model), (8, model)).T[:, :1]
    live = lax.broadcasted_iota(jnp.int32, (1, rows), 1) < counts[0]
    blocks = range(0, all_rows, rows)
    for start in blocks:
        at = slice(start, start + rows)
        inputs = points[...] if start == 0 else geometry[start - rows : start, :]
        inputs_t = inputs.T.astype(F32)
        shifted = inputs_t - jnp.mean(inputs_t, axis=0, keepdims=True)
        scale = lax.rsqrt(jnp.mean(shifted * shifted, axis=0, keepdims=True) + EPS)
        normed = (shifted * scale * gain_column).astype(BF16)
        both = dot(maps[...], normed).astype(BF16)
        normed_out[:, at] = normed
        features_out[:, at] = both[:model]
        middle_out[:, at] = both[model:]

    def logits_of(h):
        own = slice(h * width, (h + 1) * width)
        return [dot(slice_t, middle_out[own, start : start + rows]) for start in blocks]

    def numerators(h):
        own = slice(h * width, (h + 1) * width)
        cols = slice(h * slices, (h + 1) * slices)
        g, j = h // per, h % per
        for geo, (low_ref, at) in enumerate(
            ((low_out, slice(0, rows)), (geo_low_out, slice(rows, all_rows)))
        ):
            row = (geo * per + j) * width
            total[g, row : row + width, :] = dot(features_out[own, at], low_ref[cols, :], NT)

    ahead = logits_of(0)
    for h in range(heads):
        cols = slice(h * slices, (h + 1) * slices)
        logits = ahead
        if h + 1 < heads:
            ahead = logits_of(h + 1)
        factor = sharpness[h] * math.log2(math.e)
        for geo, first in ((0, 0), (1, 1)):
            weights_ref, low_ref = ((weights_out, low_out), (geo_weights_out, geo_low_out))[geo]
            folded = None
            for i in range(first, 1 if geo == 0 else len(logits)):
                for start in range(0, rows, lanes):
                    part = logits[i][:, start : start + lanes]
                    powers = jnp.exp2((part - jnp.max(part, axis=0, keepdims=True)) * factor)
                    inverse = 1.0 / jnp.sum(powers, axis=0, keepdims=True)
                    if geo == 0:
                        inverse = jnp.where(live[:, start : start + lanes], inverse, 0.0)
                    weights = powers * inverse
                    where = (i - first) * rows + start
                    weights_ref[cols, where : where + lanes] = weights
                    low_ref[cols, where : where + lanes] = weights.astype(BF16)
                    folded = weights if folded is None else folded + weights
            row = 2 * per * width + geo * per + h % per
            total[h // per, row : row + 1, :] = jnp.sum(folded.T, axis=0, keepdims=True)
        if h > 0:
            numerators(h - 1)
    numerators(heads - 1)

    place_groups(lambda g: total[g], keep, send, me & (groups - 1))


tie = lax.optimization_barrier


def token_rows(tokens, j, per, width):
    base = 2 * per * width
    out = []
    for geo in range(2):
        row = (geo * per + j) * width
        den = tokens[base + geo * per + j : base + geo * per + j + 1, :] + EPS
        out.append((tokens[row : row + width, :] / den, den))
    return out


def mix_kernel(tokens, w_query, w_key, w_value, mixed_out, attention_out, kept):
    width = w_query.shape[0]
    per = attention_out.shape[0]
    slices = tokens.shape[1]
    maps = jnp.concatenate([w_query[...], w_key[...], w_value[...]], axis=1)
    heads = range(per)
    both = [
        jnp.concatenate([part for part, _ in token_rows(tokens, j, per, width)], axis=1)
        for j in heads
    ]
    projected = [narrow_dot(maps, both[j]) for j in heads]
    for j in heads:
        kept[j] = projected[j]
    scores = [narrow_dot(projected[j][width : 2 * width], projected[j][:width, :slices]) for j in heads]
    attention = []
    for j in heads:
        scaled = (scores[j] - jnp.max(scores[j], axis=0, keepdims=True)) * (
            math.log2(math.e) / math.sqrt(width)
        )
        powers = jnp.exp2(scaled)
        attention.append(powers * (1.0 / jnp.sum(powers, axis=0, keepdims=True)))
    for j in heads:
        attention_out[j] = attention[j]
        mixed_out[j * width : (j + 1) * width, :] = wide_dot(
            projected[j][2 * width :], split(attention[j]), NN
        )


def mix_back_kernel(tokens, attention_in, kept, grad, w_query, w_key, w_value, out):
    width = w_query.shape[0]
    per, both_count, slices = attention_in.shape
    base = 2 * per * width
    small = jnp.zeros((width, 3 * width), F32)
    out[base : base + pad_to(2 * per, 8), :] = jnp.zeros((pad_to(2 * per, 8), slices), F32)
    maps_t = jnp.concatenate([w_query[...].T, w_key[...].T, w_value[...].T], axis=0)
    none = jnp.zeros((width, both_count - slices), F32)
    heads = range(per)
    rows = [token_rows(tokens, j, per, width) for j in heads]
    both = [jnp.concatenate([part for part, _ in rows[j]], axis=1) for j in heads]
    mixed_grads = [grad[j * width : (j + 1) * width, :] for j in heads]
    att_grads = [narrow_dot(kept[j, 2 * width :, :], mixed_grads[j]) for j in heads]
    value_grads = [wide_dot(mixed_grads[j], split(attention_in[j]), NT) for j in heads]
    score_grads = []
    for j in heads:
        attention = attention_in[j]
        inner = jnp.sum(attention * att_grads[j], axis=0, keepdims=True)
        score_grads.append(split(attention * (att_grads[j] - inner) * (1.0 / math.sqrt(width))))
    query_grads = [wide_dot(kept[j, width : 2 * width, :], score_grads[j], NN) for j in heads]
    key_grads = [wide_dot(kept[j, :width, :slices], score_grads[j], NT) for j in heads]
    grads = [
        jnp.concatenate(
            [jnp.concatenate([query_grads[j], none], axis=1), key_grads[j], value_grads[j]], axis=0
        )
        for j in heads
    ]
    both_grads = [narrow_dot(maps_t, grads[j]) for j in heads]
    for j in heads:
        small += wide_dot(both[j], split(grads[j]), NT)
        for g, (value_of, den) in enumerate(rows[j]):
            row = (g * per + j) * width
            scaled = both_grads[j][:, g * slices : (g + 1) * slices] / den
            out[row : row + width, :] = scaled
            out[base + g * per + j : base + g * per + j + 1, :] = -jnp.sum(
                scaled * value_of, axis=0, keepdims=True
            )
    half = width // 2
    filler = jnp.zeros((width, slices // 2 - 3 * width), F32)
    wide = jnp.concatenate([small, filler], axis=1)
    out[out.shape[0] - half :, :] = jnp.concatenate([wide[:half], wide[half:]], axis=1)


def mlp_kernel(
    rel,
    *refs,
):
    groups = len(rel)
    pieces = refs[:groups]
    (
        low,
        points,
        cotangent,
        w_out,
        gain,
        w_up,
        w_down,
        layer_out,
        grad_att_out,
        keep,
        send,
        attended,
        second_out,
        hidden_out,
        grad_upper_out,
        grad_resid_out,
        canon,
    ) = refs[groups:]
    me = lax.axis_index("pts")
    model = points.shape[1]
    slices = canon.shape[2]
    heads = low.shape[0] // slices
    width = model // heads
    per = heads // groups
    mine = me & (groups - 1)
    for r, piece in zip(rel, pieces):
        canon[mine ^ r] = piece[...]
    for h in range(heads):
        cols = slice(h * slices, (h + 1) * slices)
        j = h % per
        attended[h * width : (h + 1) * width, :] = dot(
            canon[h // per, j * width : (j + 1) * width, :].astype(BF16), low[cols, :]
        ).astype(BF16)
    gain_row = gain[...].reshape(1, model)
    residual = points[...].astype(F32) + dot(attended[...], w_out[...], TN)
    shifted, scale = norm_parts(residual)
    unit = shifted * scale
    second = (unit * gain_row).astype(BF16)
    second_out[...] = second
    upper = dot(second, w_up[...])
    square = upper * upper
    slope = jnp.tanh(GELU_A * upper * (1.0 + GELU_B * square))
    half = 0.5 * (1.0 + slope)
    hidden = (upper * half).astype(BF16)
    hidden_out[...] = hidden
    curve = half + 0.5 * upper * (1.0 - slope * slope) * (
        GELU_A * (1.0 + 3.0 * GELU_B * square)
    )
    layer_out[...] = (residual + dot(hidden, w_down[...])).astype(BF16)
    grad_upper = (dot(cotangent[...], w_down[...], NT) * curve).astype(BF16)
    grad_upper_out[...] = grad_upper
    grad_unit = dot(grad_upper, w_up[...], NT) * gain_row
    grad_norm = scale * (
        grad_unit
        - jnp.mean(grad_unit, axis=-1, keepdims=True)
        - unit * jnp.mean(grad_unit * unit, axis=-1, keepdims=True)
    )
    grad_resid = (cotangent[...].astype(F32) + grad_norm).astype(BF16)
    grad_resid_out[...] = grad_resid
    grad_att = dot(w_out[...], grad_resid, NT).astype(BF16)
    grad_att_out[...] = grad_att
    for h in range(heads):
        j = h % per
        canon[h // per, j * width : (j + 1) * width, :] = dot(
            grad_att[h * width : (h + 1) * width], low[h * slices : (h + 1) * slices, :], NT
        )
    place_groups(lambda g: canon[g], keep, send, mine)


def outer_kernel(
    order, attended, second, hidden, grad_upper, grad_resid, cotangent, keep, send, out, up, down
):
    me = lax.axis_index("pts")
    half, rows, model = keep.shape
    parts = 2 * half
    step = model // parts
    wide = hidden.shape[1] // model
    out[...] = dot(attended[...], grad_resid[...])
    up[...] = dot(second[...], grad_upper[...], TN)
    down[...] = dot(hidden[...], cotangent[...], TN)
    for pos in range(parts):
        target = keep if pos < half else send
        p = from_position(pos, order) ^ me
        i = pos % half
        at = pl.ds(pl.multiple_of(p * step, step), step)
        target[i, :step, :] = out[at, :]
        for w in range(wide):
            target[i, step * (1 + w) : step * (2 + w), :] = up[at, w * model : (w + 1) * model]
        tall = step * wide
        target[i, step * (1 + wide) :, :] = down[pl.ds(pl.multiple_of(p * tall, tall), tall), :]


def back_kernel(rel, order, sharpness, *refs):
    groups = len(rel)
    pieces = refs[:groups]
    mixed = refs[groups : 2 * groups]
    (
        weights,
        geo_weights,
        low,
        geo_low,
        features,
        middle,
        normed,
        grad_att,
        w_slice,
        keep,
        send,
        grad_mix,
        canon,
        mix_canon,
        left_field,
        left_geo,
        low_numer,
        right,
        total,
        slice_sum,
        logit,
    ) = refs[2 * groups :]
    me = lax.axis_index("pts")
    model, rows = grad_att.shape
    width, slices = w_slice.shape
    heads = model // width
    per = heads // groups
    mine = me & (groups - 1)
    base = 2 * per * width
    for r, piece, mix_piece in zip(rel, pieces, mixed):
        canon[mine ^ r] = piece[...]
        mix_canon[mine ^ r] = mix_piece[...]
    for h in range(heads):
        g, j = h // per, h % per
        for geo in range(2):
            row = (geo * per + j) * width
            numer = canon[g, row : row + width, :].astype(BF16)
            low_numer[geo, h * width : (h + 1) * width, :] = numer
            den = canon[g, base + geo * per + j : base + geo * per + j + 1, :]
            high = den.astype(BF16).astype(F32)
            middle_part = (den - high).astype(BF16).astype(F32)
            rest = den - high - middle_part
            den_rows = jnp.concatenate([high, middle_part, rest, jnp.zeros((13, slices), F32)], axis=0)
            parts = [numer.astype(F32)]
            if not geo:
                parts.append(mix_canon[g, j * width : (j + 1) * width, :])
            parts.append(den_rows)
            left = jnp.concatenate(parts, axis=0).astype(BF16).T
            if geo:
                left_geo[h] = left
            else:
                left_field[h] = left
    all_rows = normed.shape[1]
    lanes = math.gcd(rows, 128)
    ones = jnp.ones((16, rows), BF16)
    blocks = range(0, all_rows, rows)

    def products_of(h):
        own = slice(h * width, (h + 1) * width)
        out = []
        for start in blocks:
            stack = [features[own, start : start + rows]]
            if start == 0:
                stack.append(grad_att[own, :])
            left = left_field if start == 0 else left_geo
            out.append(dot(left[h], jnp.concatenate(stack + [ones], axis=0)))
        return out

    def finish(h):
        cols = slice(h * slices, (h + 1) * slices)
        own = slice(h * width, (h + 1) * width)
        right[own, :rows] = dot(low_numer[0, own, :], low[cols, :]).astype(BF16)
        right[own, rows:] = dot(low_numer[1, own, :], geo_low[cols, :]).astype(BF16)
        right[model + h * width : model + (h + 1) * width, :] = dot(
            w_slice[...], logit[cols, :]
        ).astype(BF16)
        term = dot(logit[cols, :], middle[own, :], NT)
        if h == 0:
            slice_sum[...] = term
        else:
            slice_sum[...] += term

    ahead = products_of(0)
    for h in range(heads):
        cols = slice(h * slices, (h + 1) * slices)
        products = ahead
        if h + 1 < heads:
            ahead = products_of(h + 1)
        for i, begin in enumerate(blocks):
            for start in range(0, rows, lanes):
                grad_weights = products[i][:, start : start + lanes]
                if i == 0:
                    share = weights[cols, start : start + lanes]
                else:
                    where = begin - rows + start
                    share = geo_weights[cols, where : where + lanes]
                inner = jnp.sum(share * grad_weights, axis=0, keepdims=True)
                logit[cols, begin + start : begin + start + lanes] = (
                    share * (grad_weights - inner) * sharpness[h]
                ).astype(BF16)
        if h > 0:
            finish(h - 1)
    finish(heads - 1)

    total[...] = dot(normed[...], right[...], NT)
    half = keep.shape[0] // 2
    step = model // (2 * half)
    for pos in range(2 * half):
        start = pl.multiple_of((from_position(pos, order) ^ me) * step, step)
        value = total[pl.ds(start, step), :]
        if pos < half:
            keep[2 * pos] = value[:, :model]
            keep[2 * pos + 1] = value[:, model:]
        else:
            row = (pos - half) * 2 * step
            send[row : row + step, :] = value[:, :model]
            send[row + step : row + 2 * step, :] = value[:, model:]
    send[half * 2 * step :, :] = slice_sum[...].T

    small_rows = width // 2
    packed = canon[0, canon.shape[1] - small_rows :, :]
    for g in range(1, groups):
        packed += canon[g, canon.shape[1] - small_rows :, :]
    wide = jnp.concatenate([packed[:, : slices // 2], packed[:, slices // 2 :]], axis=0)
    for i in range(3):
        grad_mix[i] = wide[:, i * width : (i + 1) * width]


def finish_kernel(keep, got, slice_sum, feat, mid, slice_out):
    step = feat.shape[0]
    feat[...] = keep[:step, :] + got[:step, :]
    mid[...] = keep[step:, :] + got[step : 2 * step, :]
    slice_out[...] = slice_sum[...] + got[2 * step :, :]


def fold_kernel(value, got, keep, send):
    count = keep.shape[0]
    keep[...] = value[:count] + got[:count]
    send[...] = value[count:] + got[count:]


def outer_finish_kernel(keep, got, out, up, down):
    step, model = out.shape
    wide = up.shape[1] // model
    out[...] = keep[0, :step, :] + got[0, :step, :]
    for w in range(wide):
        at = slice(step * (1 + w), step * (2 + w))
        up[:, w * model : (w + 1) * model] = keep[0, at, :] + got[0, at, :]
    down[...] = keep[0, step * (1 + wide) :, :] + got[0, step * (1 + wide) :, :]


VMEM = pl.BlockSpec(memory_space=pltpu.VMEM)
SMEM = pl.BlockSpec(memory_space=pltpu.SMEM)
HBM = pl.BlockSpec(memory_space=pltpu.HBM)
MIB = 1024 * 1024
COSTS = {"point_back": 0.001, "mix_back": 0.001, "fold": 8.0}


def shape(dims, dtype=F32):
    return jax.ShapeDtypeStruct(tuple(dims), dtype)


def run(body, name, limit, first, out_shape, scratch, *args):
    estimate = None
    if name in COSTS:
        estimate = pl.CostEstimate(
            flops=int(COSTS[name] * 1e9), bytes_accessed=0, transcendentals=0
        )
    rest = HBM if first is HBM else VMEM
    if first is HBM:
        args = args[:1] + tuple(
            pltpu.with_memory_space_constraint(arg, pltpu.HBM) for arg in args[1:]
        )
    return pl.pallas_call(
        body,
        out_shape=out_shape,
        in_specs=[first] + [rest] * (len(args) - 1),
        out_specs=jax.tree.map(lambda _: VMEM, out_shape),
        scratch_shapes=scratch,
        compiler_params=pltpu.CompilerParams(vmem_limit_bytes=limit * MIB),
        name=name,
        cost_estimate=estimate,
    )(*args)


def on_device(
    parts,
    points,
    geometry,
    counts,
    cotangent,
    gain_attn,
    w_feat,
    w_mid,
    w_slice,
    sharpness,
    w_query,
    w_key,
    w_value,
    w_out,
    gain_mlp,
    w_up,
    w_down,
):
    rows, model = points.shape
    geo_rows = geometry.shape[0]
    all_rows = rows + geo_rows
    width, slices = w_slice.shape
    heads = sharpness.shape[0]
    hidden_width = w_up.shape[1]
    all_bits = parts.bit_length() - 1
    bits = min(GROUP_BITS, all_bits)
    groups = 1 << bits
    per = heads // groups
    token_height = 2 * per * width + pad_to(2 * per, 8)
    grad_height = token_height + width // 2
    half = groups // 2
    step = model // parts
    wide = hidden_width // model

    def exchange(value, bit):
        return lax.ppermute(value, "pts", [(i, i ^ (1 << bit)) for i in range(parts)])

    def fold(keep, got):
        count = keep.shape[0] // 2
        return keep[:count] + got[:count], keep[count:] + got[count:]

    def add_all(value, first, last):
        for bit in range(first, last):
            value = value + exchange(value, bit)
        return value

    def collect(pieces, first, count):
        for bit in reversed(range(first, first + count)):
            pieces = pieces + [exchange(piece, bit) for piece in pieces]
        return pieces

    main_order = outer_order = (0, 2, 1) + tuple(range(3, all_bits))
    rel = [0]
    for bit in reversed(range(bits)):
        rel = rel + [r ^ (1 << bit) for r in rel]

    keep, send, normed, features, middle, weights, geo_weights, low, geo_low = run(
        sums_kernel,
        "slice_sums",
        20,
        HBM,
        (
            shape((half, token_height, slices)),
            shape((half, token_height, slices)),
            shape((model, all_rows), BF16),
            shape((model, all_rows), BF16),
            shape((model, all_rows), BF16),
            shape((heads * slices, rows)),
            shape((heads * slices, geo_rows)),
            shape((heads * slices, rows), BF16),
            shape((heads * slices, geo_rows), BF16),
        ),
        [
            pltpu.VMEM((groups, token_height, slices), F32),
            pltpu.VMEM((2 * model, model), BF16),
            pltpu.SMEM(counts.shape, jnp.int32),
            pltpu.SMEM(sharpness.shape, F32),
            pltpu.VMEM(points.shape, BF16),
            pltpu.VMEM(geometry.shape, BF16),
            pltpu.VMEM(gain_attn.shape, F32),
            pltpu.VMEM(w_feat.shape, BF16),
            pltpu.VMEM(w_mid.shape, BF16),
            pltpu.VMEM(w_slice.shape, BF16),
            pltpu.SemaphoreType.DMA((8,)),
        ],
        counts,
        sharpness,
        points,
        geometry,
        gain_attn,
        w_feat,
        w_mid,
        w_slice,
    )
    got = exchange(send, 0)
    for bit in range(1, bits):
        keep, send = fold(keep, got)
        got = exchange(send, bit)
    tokens = add_all((keep + got)[0], bits, all_bits)
    mixed, attention, kept = run(
        mix_kernel,
        "mix_tokens",
        12,
        VMEM,
        (
            shape((per * width, slices)),
            shape((per, 2 * slices, slices)),
            shape((per, 3 * width, 2 * slices)),
        ),
        [],
        tokens,
        w_query,
        w_key,
        w_value,
    )
    mixed_pieces = collect([mixed], 0, bits)
    (
        layer_out,
        grad_att,
        keep,
        send,
        attended,
        second,
        hidden,
        grad_upper,
        grad_resid,
    ) = run(
        functools.partial(mlp_kernel, tuple(rel)),
        "mlp",
        24,
        VMEM,
        (
            shape((rows, model), BF16),
            shape((model, rows), BF16),
            shape((half, per * width, slices)),
            shape((half, per * width, slices)),
            shape((model, rows), BF16),
            shape((rows, model), BF16),
            shape((rows, hidden_width), BF16),
            shape((rows, hidden_width), BF16),
            shape((rows, model), BF16),
        ),
        [pltpu.VMEM((groups, per * width, slices), F32)],
        *mixed_pieces,
        low,
        points,
        cotangent,
        w_out,
        gain_mlp,
        w_up,
        w_down,
    )
    got = exchange(send, 0)
    attended, second, hidden, grad_upper, grad_resid, got = tie(
        (attended, second, hidden, grad_upper, grad_resid, got)
    )
    outer_keep, outer_send = run(
        functools.partial(outer_kernel, outer_order),
        "weight_grads",
        16,
        VMEM,
        (shape((parts // 2, step * (1 + 2 * wide), model)),) * 2,
        [
            pltpu.VMEM((model, model), F32),
            pltpu.VMEM((model, hidden_width), F32),
            pltpu.VMEM((hidden_width, model), F32),
        ],
        attended,
        second,
        hidden,
        grad_upper,
        grad_resid,
        cotangent,
    )
    for bit in range(1, bits):
        keep, send = fold(keep, got)
        got = exchange(send, bit)
    outer_got = exchange(outer_send, 0)
    mixed_grad = add_all((keep + got)[0], bits, all_bits)
    mixed_grad, outer_got = tie((mixed_grad, outer_got))
    outer_keep, outer_send = fold(outer_keep, outer_got)
    outer_got = exchange(outer_send, outer_order[1])
    token_grad = run(
        mix_back_kernel,
        "mix_back",
        16,
        VMEM,
        shape((grad_height, slices)),
        [],
        tokens,
        attention,
        kept,
        mixed_grad,
        w_query,
        w_key,
        w_value,
    )
    grad_pieces = collect([token_grad], 0, bits)
    keep, send, grad_mix = run(
        functools.partial(back_kernel, tuple(rel), main_order),
        "point_back",
        24,
        SMEM,
        (
            shape((parts, step, model)),
            shape((parts * step + width, model)),
            shape((3, width, width)),
        ),
        [
            pltpu.VMEM((groups, grad_height, slices), F32),
            pltpu.VMEM((groups, per * width, slices), F32),
            pltpu.VMEM((heads, slices, 2 * width + 16), BF16),
            pltpu.VMEM((heads, slices, width + 16), BF16),
            pltpu.VMEM((2, model, slices), BF16),
            pltpu.VMEM((2 * model, all_rows), BF16),
            pltpu.VMEM((model, 2 * model), F32),
            pltpu.VMEM((slices, width), F32),
            pltpu.VMEM((heads * slices, all_rows), BF16),
        ],
        sharpness,
        *grad_pieces,
        *mixed_pieces,
        weights,
        geo_weights,
        low,
        geo_low,
        features,
        middle,
        normed,
        grad_att,
        w_slice,
    )
    keep = keep.reshape(-1, model)
    slice_sum = send[keep.shape[0] :]
    for turn, bit in enumerate(main_order):
        if turn == 0:
            send, outer_got = tie((send, outer_got))
            outer_keep, outer_send = fold(outer_keep, outer_got)
            outer_got = exchange(outer_send, outer_order[2])
            send, outer_keep = tie((send, outer_keep))
        if turn == 2:
            count = outer_keep.shape[0] // 2
            outer_keep, outer_send = run(
                fold_kernel,
                "fold",
                4,
                VMEM,
                (shape((count,) + outer_keep.shape[1:]),) * 2,
                [],
                outer_keep,
                outer_got,
            )
            send, outer_keep = tie((send, outer_keep))
            outer_got = exchange(outer_send, outer_order[3])
        got = exchange(send, bit)
        if turn == all_bits - 1:
            break
        slice_sum = slice_sum + got[keep.shape[0] :]
        count = keep.shape[0] // 2
        send = jnp.concatenate([keep[count:] + got[count : 2 * count], slice_sum], axis=0)
        keep = keep[:count] + got[:count]
    grad_feat, grad_mid, grad_slice = run(
        finish_kernel,
        "finish",
        4,
        VMEM,
        (shape((step, model)), shape((step, model)), shape((width, slices))),
        [],
        keep,
        got,
        slice_sum,
    )
    for bit in outer_order[4:]:
        outer_keep, outer_send = fold(outer_keep, outer_got)
        outer_got = exchange(outer_send, bit)
    grad_out, grad_up, grad_down = run(
        outer_finish_kernel,
        "outer_finish",
        4,
        VMEM,
        (shape((step, model)), shape((step, hidden_width)), shape((step * wide, model))),
        [],
        outer_keep,
        outer_got,
    )
    return (layer_out, grad_feat, grad_mid, grad_out, grad_up, grad_down, grad_slice, grad_mix)


def solution(mesh):
    split = P(("design", "pts"), None)
    placed = (split, split, P(("design", "pts")), split) + (P(),) * 12
    return jax.shard_map(
        functools.partial(on_device, mesh.shape["pts"]),
        mesh=mesh,
        in_specs=placed,
        out_specs=(split,) * 6 + (P("design", None), P("design", None, None)),
        check_vma=False,
    )
```

```python
import functools
import math

import jax
import jax.numpy as jnp
from jax import lax
from jax.experimental import pallas as pl
from jax.experimental.pallas import tpu as pltpu
from jax.sharding import PartitionSpec as P

F32 = jnp.float32
BF16 = jnp.bfloat16
EPS = 1e-05
GROUP_BITS = (0, 2)
GELU_A = math.sqrt(2.0 / math.pi)
GELU_B = 0.044715

NN = ((1,), (0,))
NT = ((1,), (1,))
TN = ((0,), (0,))


def dot(left, right, dims=NN, precision=None):
    return lax.dot_general(
        left, right, (dims, ((), ())), precision=precision, preferred_element_type=F32
    )


def bit_reverse(value, bits):
    out = 0
    for k in range(bits):
        out = (out << 1) | ((value >> k) & 1)
    return out


def group_of(me):
    out = 0
    for k, bit in enumerate(GROUP_BITS):
        out |= ((me >> bit) & 1) << k
    return out


def from_position(pos, order):
    out = 0
    for i, bit in enumerate(order):
        out |= ((pos >> (len(order) - 1 - i)) & 1) << bit
    return out


def norm_parts(inputs):
    centre = jnp.mean(inputs, axis=-1, keepdims=True)
    shifted = inputs - centre
    spread = jnp.mean(shifted * shifted, axis=-1, keepdims=True)
    return shifted, lax.rsqrt(spread + EPS)


def pad_to(count, unit):
    return -(-count // unit) * unit


def split(value):
    high = value.astype(BF16)
    return high, (value - high.astype(F32)).astype(BF16)


def narrow_dot(left, right):
    left_high, left_low = split(left)
    right_high, right_low = split(right)
    return dot(
        jnp.concatenate([left_high, left_high, left_low], axis=0),
        jnp.concatenate([right_high, right_low, right_high], axis=0),
        TN,
    )


def wide_dot(left, right_parts, dims):
    rows = left.shape[0]
    high, low = split(left)
    right_high, right_low = right_parts
    both = dot(jnp.concatenate([high, low], axis=0), right_high, dims)
    return both[:rows] + both[rows:] + dot(high, right_low, dims)


def place_groups(value_of, keep, send, mine):
    half = keep.shape[0]
    bits = (2 * half).bit_length() - 1
    for pos in range(2 * half):
        target = keep if pos < half else send
        target[pos % half] = value_of(bit_reverse(pos, bits) ^ mine)


def sums_kernel(
    counts_hbm,
    sharpness_hbm,
    points_hbm,
    geometry_hbm,
    gain_hbm,
    w_feat_hbm,
    w_mid_hbm,
    w_slice_hbm,
    keep,
    send,
    normed_out,
    features_out,
    middle_out,
    weights_out,
    geo_weights_out,
    low_out,
    geo_low_out,
    total,
    maps,
    counts,
    sharpness,
    points,
    geometry,
    gain,
    w_feat,
    w_mid,
    w_slice,
    sems,
):
    copies = [
        pltpu.make_async_copy(source, target, sems.at[i])
        for i, (source, target) in enumerate(
            (
                (points_hbm, points),
                (geometry_hbm, geometry),
                (w_feat_hbm, w_feat),
                (w_mid_hbm, w_mid),
                (gain_hbm, gain),
                (w_slice_hbm, w_slice),
                (sharpness_hbm, sharpness),
                (counts_hbm, counts),
            )
        )
    ]
    for copy in copies:
        copy.start()
    me = lax.axis_index("pts")
    rows, model = points.shape
    all_rows = rows + geometry.shape[0]
    width, slices = w_slice.shape
    heads = model // width
    groups = total.shape[0]
    per = heads // groups
    lanes = math.gcd(rows, 128)
    filled = 2 * per * (width + 1)
    total[:, filled:, :] = jnp.zeros((groups, total.shape[1] - filled, slices), F32)
    for copy in copies:
        copy.wait()
    slice_t = w_slice[...].T
    maps[:model, :] = w_feat[...].T
    maps[model:, :] = w_mid[...].T
    gain_column = jnp.broadcast_to(gain[...].reshape(1, model), (8, model)).T[:, :1]
    live = lax.broadcasted_iota(jnp.int32, (1, rows), 1) < counts[0]
    blocks = range(0, all_rows, rows)
    for start in blocks:
        at = slice(start, start + rows)
        inputs = points[...] if start == 0 else geometry[start - rows : start, :]
        inputs_t = inputs.T.astype(F32)
        shifted = inputs_t - jnp.mean(inputs_t, axis=0, keepdims=True)
        scale = lax.rsqrt(jnp.mean(shifted * shifted, axis=0, keepdims=True) + EPS)
        normed = (shifted * scale * gain_column).astype(BF16)
        both = dot(maps[...], normed).astype(BF16)
        normed_out[:, at] = normed
        features_out[:, at] = both[:model]
        middle_out[:, at] = both[model:]

    def logits_of(h):
        own = slice(h * width, (h + 1) * width)
        return [dot(slice_t, middle_out[own, start : start + rows]) for start in blocks]

    def numerators(h):
        own = slice(h * width, (h + 1) * width)
        cols = slice(h * slices, (h + 1) * slices)
        g, j = h // per, h % per
        for geo, (low_ref, at) in enumerate(
            ((low_out, slice(0, rows)), (geo_low_out, slice(rows, all_rows)))
        ):
            row = (geo * per + j) * width
            total[g, row : row + width, :] = dot(features_out[own, at], low_ref[cols, :], NT)

    ahead = logits_of(0)
    for h in range(heads):
        cols = slice(h * slices, (h + 1) * slices)
        logits = ahead
        if h + 1 < heads:
            ahead = logits_of(h + 1)
        factor = sharpness[h] * math.log2(math.e)
        for geo, first in ((0, 0), (1, 1)):
            weights_ref, low_ref = ((weights_out, low_out), (geo_weights_out, geo_low_out))[geo]
            folded = None
            for i in range(first, 1 if geo == 0 else len(logits)):
                for start in range(0, rows, lanes):
                    part = logits[i][:, start : start + lanes]
                    powers = jnp.exp2((part - jnp.max(part, axis=0, keepdims=True)) * factor)
                    inverse = 1.0 / jnp.sum(powers, axis=0, keepdims=True)
                    if geo == 0:
                        inverse = jnp.where(live[:, start : start + lanes], inverse, 0.0)
                    weights = powers * inverse
                    where = (i - first) * rows + start
                    weights_ref[cols, where : where + lanes] = weights
                    low_ref[cols, where : where + lanes] = weights.astype(BF16)
                    folded = weights if folded is None else folded + weights
            row = 2 * per * width + geo * per + h % per
            total[h // per, row : row + 1, :] = jnp.sum(folded.T, axis=0, keepdims=True)
        if h > 0:
            numerators(h - 1)
    numerators(heads - 1)

    place_groups(lambda g: total[g], keep, send, group_of(me))


tie = lax.optimization_barrier


def token_rows(tokens, j, per, width):
    base = 2 * per * width
    out = []
    for geo in range(2):
        row = (geo * per + j) * width
        den = tokens[base + geo * per + j : base + geo * per + j + 1, :] + EPS
        out.append((tokens[row : row + width, :] / den, den))
    return out


def mix_kernel(tokens, w_query, w_key, w_value, mixed_out, attention_out, kept):
    width = w_query.shape[0]
    per = attention_out.shape[0]
    slices = tokens.shape[1]
    maps = jnp.concatenate([w_query[...], w_key[...], w_value[...]], axis=1)
    heads = range(per)
    both = [
        jnp.concatenate([part for part, _ in token_rows(tokens, j, per, width)], axis=1)
        for j in heads
    ]
    projected = [narrow_dot(maps, both[j]) for j in heads]
    for j in heads:
        kept[j] = projected[j]
    scores = [narrow_dot(projected[j][width : 2 * width], projected[j][:width, :slices]) for j in heads]
    attention = []
    for j in heads:
        scaled = (scores[j] - jnp.max(scores[j], axis=0, keepdims=True)) * (
            math.log2(math.e) / math.sqrt(width)
        )
        powers = jnp.exp2(scaled)
        attention.append(powers * (1.0 / jnp.sum(powers, axis=0, keepdims=True)))
    for j in heads:
        attention_out[j] = attention[j]
        mixed_out[j * width : (j + 1) * width, :] = wide_dot(
            projected[j][2 * width :], split(attention[j]), NN
        )


def mix_back_kernel(tokens, attention_in, kept, grad, w_query, w_key, w_value, out):
    width = w_query.shape[0]
    per, both_count, slices = attention_in.shape
    base = 2 * per * width
    small = jnp.zeros((width, 3 * width), F32)
    out[base : base + pad_to(2 * per, 8), :] = jnp.zeros((pad_to(2 * per, 8), slices), F32)
    maps_t = jnp.concatenate([w_query[...].T, w_key[...].T, w_value[...].T], axis=0)
    none = jnp.zeros((width, both_count - slices), F32)
    heads = range(per)
    rows = [token_rows(tokens, j, per, width) for j in heads]
    both = [jnp.concatenate([part for part, _ in rows[j]], axis=1) for j in heads]
    mixed_grads = [grad[j * width : (j + 1) * width, :] for j in heads]
    att_grads = [narrow_dot(kept[j, 2 * width :, :], mixed_grads[j]) for j in heads]
    value_grads = [wide_dot(mixed_grads[j], split(attention_in[j]), NT) for j in heads]
    score_grads = []
    for j in heads:
        attention = attention_in[j]
        inner = jnp.sum(attention * att_grads[j], axis=0, keepdims=True)
        score_grads.append(split(attention * (att_grads[j] - inner) * (1.0 / math.sqrt(width))))
    query_grads = [wide_dot(kept[j, width : 2 * width, :], score_grads[j], NN) for j in heads]
    key_grads = [wide_dot(kept[j, :width, :slices], score_grads[j], NT) for j in heads]
    grads = [
        jnp.concatenate(
            [jnp.concatenate([query_grads[j], none], axis=1), key_grads[j], value_grads[j]], axis=0
        )
        for j in heads
    ]
    both_grads = [narrow_dot(maps_t, grads[j]) for j in heads]
    for j in heads:
        small += wide_dot(both[j], split(grads[j]), NT)
        for g, (value_of, den) in enumerate(rows[j]):
            row = (g * per + j) * width
            scaled = both_grads[j][:, g * slices : (g + 1) * slices] / den
            out[row : row + width, :] = scaled
            out[base + g * per + j : base + g * per + j + 1, :] = -jnp.sum(
                scaled * value_of, axis=0, keepdims=True
            )
    half = width // 2
    filler = jnp.zeros((width, slices // 2 - 3 * width), F32)
    wide = jnp.concatenate([small, filler], axis=1)
    out[out.shape[0] - half :, :] = jnp.concatenate([wide[:half], wide[half:]], axis=1)


def mlp_kernel(
    rel,
    *refs,
):
    groups = len(rel)
    pieces = refs[:groups]
    (
        low,
        points,
        cotangent,
        w_out,
        gain,
        w_up,
        w_down,
        layer_out,
        grad_att_out,
        keep,
        send,
        attended,
        second_out,
        hidden_out,
        grad_upper_out,
        grad_resid_out,
        canon,
    ) = refs[groups:]
    me = lax.axis_index("pts")
    model = points.shape[1]
    slices = canon.shape[2]
    heads = low.shape[0] // slices
    width = model // heads
    per = heads // groups
    mine = group_of(me)
    for r, piece in zip(rel, pieces):
        canon[mine ^ r] = piece[...]
    for h in range(heads):
        cols = slice(h * slices, (h + 1) * slices)
        j = h % per
        attended[h * width : (h + 1) * width, :] = dot(
            canon[h // per, j * width : (j + 1) * width, :].astype(BF16), low[cols, :]
        ).astype(BF16)
    gain_row = gain[...].reshape(1, model)
    residual = points[...].astype(F32) + dot(attended[...], w_out[...], TN)
    shifted, scale = norm_parts(residual)
    unit = shifted * scale
    second = (unit * gain_row).astype(BF16)
    second_out[...] = second
    upper = dot(second, w_up[...])
    square = upper * upper
    slope = jnp.tanh(GELU_A * upper * (1.0 + GELU_B * square))
    half = 0.5 * (1.0 + slope)
    hidden = (upper * half).astype(BF16)
    hidden_out[...] = hidden
    curve = half + 0.5 * upper * (1.0 - slope * slope) * (
        GELU_A * (1.0 + 3.0 * GELU_B * square)
    )
    layer_out[...] = (residual + dot(hidden, w_down[...])).astype(BF16)
    grad_upper = (dot(cotangent[...], w_down[...], NT) * curve).astype(BF16)
    grad_upper_out[...] = grad_upper
    grad_unit = dot(grad_upper, w_up[...], NT) * gain_row
    grad_norm = scale * (
        grad_unit
        - jnp.mean(grad_unit, axis=-1, keepdims=True)
        - unit * jnp.mean(grad_unit * unit, axis=-1, keepdims=True)
    )
    grad_resid = (cotangent[...].astype(F32) + grad_norm).astype(BF16)
    grad_resid_out[...] = grad_resid
    grad_att = dot(w_out[...], grad_resid, NT).astype(BF16)
    grad_att_out[...] = grad_att
    for h in range(heads):
        j = h % per
        canon[h // per, j * width : (j + 1) * width, :] = dot(
            grad_att[h * width : (h + 1) * width], low[h * slices : (h + 1) * slices, :], NT
        )
    place_groups(lambda g: canon[g], keep, send, mine)


def outer_kernel(
    order, attended, second, hidden, grad_upper, grad_resid, cotangent, keep, send, out, up, down
):
    me = lax.axis_index("pts")
    half, rows, model = keep.shape
    parts = 2 * half
    step = model // parts
    wide = hidden.shape[1] // model
    out[...] = dot(attended[...], grad_resid[...])
    up[...] = dot(second[...], grad_upper[...], TN)
    down[...] = dot(hidden[...], cotangent[...], TN)
    for pos in range(parts):
        target = keep if pos < half else send
        p = from_position(pos, order) ^ me
        i = pos % half
        at = pl.ds(pl.multiple_of(p * step, step), step)
        target[i, :step, :] = out[at, :]
        for w in range(wide):
            target[i, step * (1 + w) : step * (2 + w), :] = up[at, w * model : (w + 1) * model]
        tall = step * wide
        target[i, step * (1 + wide) :, :] = down[pl.ds(pl.multiple_of(p * tall, tall), tall), :]


def back_kernel(rel, order, sharpness, *refs):
    groups = len(rel)
    pieces = refs[:groups]
    mixed = refs[groups : 2 * groups]
    (
        weights,
        geo_weights,
        low,
        geo_low,
        features,
        middle,
        normed,
        grad_att,
        w_slice,
        keep,
        send,
        grad_mix,
        canon,
        mix_canon,
        left_field,
        left_geo,
        low_numer,
        right,
        total,
        slice_sum,
        logit,
    ) = refs[2 * groups :]
    me = lax.axis_index("pts")
    model, rows = grad_att.shape
    width, slices = w_slice.shape
    heads = model // width
    per = heads // groups
    mine = group_of(me)
    base = 2 * per * width
    for r, piece, mix_piece in zip(rel, pieces, mixed):
        canon[mine ^ r] = piece[...]
        mix_canon[mine ^ r] = mix_piece[...]
    for h in range(heads):
        g, j = h // per, h % per
        for geo in range(2):
            row = (geo * per + j) * width
            numer = canon[g, row : row + width, :].astype(BF16)
            low_numer[geo, h * width : (h + 1) * width, :] = numer
            den = canon[g, base + geo * per + j : base + geo * per + j + 1, :]
            high = den.astype(BF16).astype(F32)
            middle_part = (den - high).astype(BF16).astype(F32)
            rest = den - high - middle_part
            den_rows = jnp.concatenate([high, middle_part, rest, jnp.zeros((13, slices), F32)], axis=0)
            parts = [numer.astype(F32)]
            if not geo:
                parts.append(mix_canon[g, j * width : (j + 1) * width, :])
            parts.append(den_rows)
            left = jnp.concatenate(parts, axis=0).astype(BF16).T
            if geo:
                left_geo[h] = left
            else:
                left_field[h] = left
    all_rows = normed.shape[1]
    lanes = math.gcd(rows, 128)
    ones = jnp.ones((16, rows), BF16)
    blocks = range(0, all_rows, rows)

    def products_of(h):
        own = slice(h * width, (h + 1) * width)
        out = []
        for start in blocks:
            stack = [features[own, start : start + rows]]
            if start == 0:
                stack.append(grad_att[own, :])
            left = left_field if start == 0 else left_geo
            out.append(dot(left[h], jnp.concatenate(stack + [ones], axis=0)))
        return out

    def finish(h):
        cols = slice(h * slices, (h + 1) * slices)
        own = slice(h * width, (h + 1) * width)
        right[own, :rows] = dot(low_numer[0, own, :], low[cols, :]).astype(BF16)
        right[own, rows:] = dot(low_numer[1, own, :], geo_low[cols, :]).astype(BF16)
        right[model + h * width : model + (h + 1) * width, :] = dot(
            w_slice[...], logit[cols, :]
        ).astype(BF16)
        term = dot(logit[cols, :], middle[own, :], NT)
        if h == 0:
            slice_sum[...] = term
        else:
            slice_sum[...] += term

    ahead = products_of(0)
    for h in range(heads):
        cols = slice(h * slices, (h + 1) * slices)
        products = ahead
        if h + 1 < heads:
            ahead = products_of(h + 1)
        for i, begin in enumerate(blocks):
            for start in range(0, rows, lanes):
                grad_weights = products[i][:, start : start + lanes]
                if i == 0:
                    share = weights[cols, start : start + lanes]
                else:
                    where = begin - rows + start
                    share = geo_weights[cols, where : where + lanes]
                inner = jnp.sum(share * grad_weights, axis=0, keepdims=True)
                logit[cols, begin + start : begin + start + lanes] = (
                    share * (grad_weights - inner) * sharpness[h]
                ).astype(BF16)
        if h > 0:
            finish(h - 1)
    finish(heads - 1)

    total[...] = dot(normed[...], right[...], NT)
    half = keep.shape[0] // 2
    step = model // (2 * half)
    for pos in range(2 * half):
        start = pl.multiple_of((from_position(pos, order) ^ me) * step, step)
        value = total[pl.ds(start, step), :]
        if pos < half:
            keep[2 * pos] = value[:, :model]
            keep[2 * pos + 1] = value[:, model:]
        else:
            row = (pos - half) * 2 * step
            send[row : row + step, :] = value[:, :model]
            send[row + step : row + 2 * step, :] = value[:, model:]
    send[half * 2 * step :, :] = slice_sum[...].T

    small_rows = width // 2
    packed = canon[0, canon.shape[1] - small_rows :, :]
    for g in range(1, groups):
        packed += canon[g, canon.shape[1] - small_rows :, :]
    wide = jnp.concatenate([packed[:, : slices // 2], packed[:, slices // 2 :]], axis=0)
    for i in range(3):
        grad_mix[i] = wide[:, i * width : (i + 1) * width]


def add_kernel(left, right, out):
    out[...] = left[...] + right[...]


def finish_kernel(main_keep, main_got, slice_sum, value, feat, mid, slice_out, out, up, down):
    step, model = out.shape
    feat[...] = main_keep[:step, :] + main_got[:step, :]
    mid[...] = main_keep[step:, :] + main_got[step : 2 * step, :]
    slice_out[...] = slice_sum[...] + main_got[2 * step :, :]
    wide = up.shape[1] // model
    out[...] = value[0, :step, :]
    for w in range(wide):
        at = slice(step * (1 + w), step * (2 + w))
        up[:, w * model : (w + 1) * model] = value[0, at, :]
    down[...] = value[0, step * (1 + wide) :, :]


VMEM = pl.BlockSpec(memory_space=pltpu.VMEM)
SMEM = pl.BlockSpec(memory_space=pltpu.SMEM)
HBM = pl.BlockSpec(memory_space=pltpu.HBM)
MIB = 1024 * 1024
COSTS = {"point_back": 0.001, "mix_back": 0.001, "add": 12.0}


def shape(dims, dtype=F32):
    return jax.ShapeDtypeStruct(tuple(dims), dtype)


def run(body, name, limit, first, out_shape, scratch, *args):
    estimate = None
    if name in COSTS:
        estimate = pl.CostEstimate(
            flops=int(COSTS[name] * 1e9), bytes_accessed=0, transcendentals=0
        )
    rest = HBM if first is HBM else VMEM
    if first is HBM:
        args = args[:1] + tuple(
            pltpu.with_memory_space_constraint(arg, pltpu.HBM) for arg in args[1:]
        )
    return pl.pallas_call(
        body,
        out_shape=out_shape,
        in_specs=[first] + [rest] * (len(args) - 1),
        out_specs=jax.tree.map(lambda _: VMEM, out_shape),
        scratch_shapes=scratch,
        compiler_params=pltpu.CompilerParams(vmem_limit_bytes=limit * MIB),
        name=name,
        cost_estimate=estimate,
    )(*args)


def on_device(
    parts,
    points,
    geometry,
    counts,
    cotangent,
    gain_attn,
    w_feat,
    w_mid,
    w_slice,
    sharpness,
    w_query,
    w_key,
    w_value,
    w_out,
    gain_mlp,
    w_up,
    w_down,
):
    rows, model = points.shape
    geo_rows = geometry.shape[0]
    all_rows = rows + geo_rows
    width, slices = w_slice.shape
    heads = sharpness.shape[0]
    hidden_width = w_up.shape[1]
    all_bits = parts.bit_length() - 1
    bits = len(GROUP_BITS)
    rest_bits = [bit for bit in range(all_bits) if bit not in GROUP_BITS]
    groups = 1 << bits
    per = heads // groups
    token_height = 2 * per * width + pad_to(2 * per, 8)
    grad_height = token_height + width // 2
    half = groups // 2
    step = model // parts
    wide = hidden_width // model

    def exchange(value, bit):
        return lax.ppermute(value, "pts", [(i, i ^ (1 << bit)) for i in range(parts)])

    def fold(keep, got):
        count = keep.shape[0] // 2
        return keep[:count] + got[:count], keep[count:] + got[count:]

    def add_all(value, over):
        for bit in over:
            value = value + exchange(value, bit)
        return value

    def collect(pieces):
        for bit in reversed(GROUP_BITS):
            pieces = pieces + [exchange(piece, bit) for piece in pieces]
        return pieces

    main_order = outer_order = tuple(range(all_bits))
    rel = [0]
    for bit in reversed(range(bits)):
        rel = rel + [r ^ (1 << bit) for r in rel]

    keep, send, normed, features, middle, weights, geo_weights, low, geo_low = run(
        sums_kernel,
        "slice_sums",
        20,
        HBM,
        (
            shape((half, token_height, slices)),
            shape((half, token_height, slices)),
            shape((model, all_rows), BF16),
            shape((model, all_rows), BF16),
            shape((model, all_rows), BF16),
            shape((heads * slices, rows)),
            shape((heads * slices, geo_rows)),
            shape((heads * slices, rows), BF16),
            shape((heads * slices, geo_rows), BF16),
        ),
        [
            pltpu.VMEM((groups, token_height, slices), F32),
            pltpu.VMEM((2 * model, model), BF16),
            pltpu.SMEM(counts.shape, jnp.int32),
            pltpu.SMEM(sharpness.shape, F32),
            pltpu.VMEM(points.shape, BF16),
            pltpu.VMEM(geometry.shape, BF16),
            pltpu.VMEM(gain_attn.shape, F32),
            pltpu.VMEM(w_feat.shape, BF16),
            pltpu.VMEM(w_mid.shape, BF16),
            pltpu.VMEM(w_slice.shape, BF16),
            pltpu.SemaphoreType.DMA((8,)),
        ],
        counts,
        sharpness,
        points,
        geometry,
        gain_attn,
        w_feat,
        w_mid,
        w_slice,
    )
    got = exchange(send, GROUP_BITS[0])
    for bit in GROUP_BITS[1:]:
        keep, send = fold(keep, got)
        got = exchange(send, bit)
    tokens = add_all((keep + got)[0], rest_bits)
    mixed, attention, kept = run(
        mix_kernel,
        "mix_tokens",
        12,
        VMEM,
        (
            shape((per * width, slices)),
            shape((per, 2 * slices, slices)),
            shape((per, 3 * width, 2 * slices)),
        ),
        [],
        tokens,
        w_query,
        w_key,
        w_value,
    )
    mixed_pieces = collect([mixed])
    (
        layer_out,
        grad_att,
        keep,
        send,
        attended,
        second,
        hidden,
        grad_upper,
        grad_resid,
    ) = run(
        functools.partial(mlp_kernel, tuple(rel)),
        "mlp",
        24,
        VMEM,
        (
            shape((rows, model), BF16),
            shape((model, rows), BF16),
            shape((half, per * width, slices)),
            shape((half, per * width, slices)),
            shape((model, rows), BF16),
            shape((rows, model), BF16),
            shape((rows, hidden_width), BF16),
            shape((rows, hidden_width), BF16),
            shape((rows, model), BF16),
        ),
        [pltpu.VMEM((groups, per * width, slices), F32)],
        *mixed_pieces,
        low,
        points,
        cotangent,
        w_out,
        gain_mlp,
        w_up,
        w_down,
    )
    got = exchange(send, GROUP_BITS[0])
    attended, second, hidden, grad_upper, grad_resid, got = tie(
        (attended, second, hidden, grad_upper, grad_resid, got)
    )
    outer_keep, outer_send = run(
        functools.partial(outer_kernel, outer_order),
        "weight_grads",
        16,
        VMEM,
        (shape((parts // 2, step * (1 + 2 * wide), model)),) * 2,
        [
            pltpu.VMEM((model, model), F32),
            pltpu.VMEM((model, hidden_width), F32),
            pltpu.VMEM((hidden_width, model), F32),
        ],
        attended,
        second,
        hidden,
        grad_upper,
        grad_resid,
        cotangent,
    )
    for bit in GROUP_BITS[1:]:
        keep, send = fold(keep, got)
        got = exchange(send, bit)
    outer_got = exchange(outer_send, outer_order[0])
    mixed_grad = add_all((keep + got)[0], rest_bits[:1])
    mixed_grad, outer_got = tie((mixed_grad, outer_got))
    outer_keep, outer_send = fold(outer_keep, outer_got)
    outer_got = exchange(outer_send, outer_order[1])
    mixed_grad = add_all(mixed_grad, rest_bits[1:])
    token_grad = run(
        mix_back_kernel,
        "mix_back",
        16,
        VMEM,
        shape((grad_height, slices)),
        [],
        tokens,
        attention,
        kept,
        mixed_grad,
        w_query,
        w_key,
        w_value,
    )
    grad_pieces = collect([token_grad])
    outer_keep, outer_send = fold(outer_keep, outer_got)
    outer_got = exchange(outer_send, outer_order[2])
    keep, send, grad_mix = run(
        functools.partial(back_kernel, tuple(rel), main_order),
        "point_back",
        24,
        SMEM,
        (
            shape((parts, step, model)),
            shape((parts * step + width, model)),
            shape((3, width, width)),
        ),
        [
            pltpu.VMEM((groups, grad_height, slices), F32),
            pltpu.VMEM((groups, per * width, slices), F32),
            pltpu.VMEM((heads, slices, 2 * width + 16), BF16),
            pltpu.VMEM((heads, slices, width + 16), BF16),
            pltpu.VMEM((2, model, slices), BF16),
            pltpu.VMEM((2 * model, all_rows), BF16),
            pltpu.VMEM((model, 2 * model), F32),
            pltpu.VMEM((slices, width), F32),
            pltpu.VMEM((heads * slices, all_rows), BF16),
        ],
        sharpness,
        *grad_pieces,
        *mixed_pieces,
        weights,
        geo_weights,
        low,
        geo_low,
        features,
        middle,
        normed,
        grad_att,
        w_slice,
    )
    keep = keep.reshape(-1, model)
    slice_sum = send[keep.shape[0] :]
    for turn, bit in enumerate(main_order):
        if turn == 0:
            send, outer_got = tie((send, outer_got))
            outer_keep, outer_send = fold(outer_keep, outer_got)
            outer_got = exchange(outer_send, outer_order[3])
        if turn == all_bits - 1:
            for late in outer_order[4:]:
                outer_keep, outer_send = fold(outer_keep, outer_got)
                outer_got = exchange(outer_send, late)
            outer = run(
                add_kernel, "add", 4, VMEM, shape(outer_keep.shape), [], outer_keep, outer_got
            )
            send, outer = tie((send, outer))
        got = exchange(send, bit)
        if turn == all_bits - 1:
            break
        slice_sum = slice_sum + got[keep.shape[0] :]
        count = keep.shape[0] // 2
        send = jnp.concatenate([keep[count:] + got[count : 2 * count], slice_sum], axis=0)
        keep = keep[:count] + got[:count]
    grad_feat, grad_mid, grad_slice, grad_out, grad_up, grad_down = run(
        finish_kernel,
        "finish",
        4,
        VMEM,
        (
            shape((step, model)),
            shape((step, model)),
            shape((width, slices)),
            shape((step, model)),
            shape((step, hidden_width)),
            shape((step * wide, model)),
        ),
        [],
        keep,
        got,
        slice_sum,
        outer,
    )
    return (layer_out, grad_feat, grad_mid, grad_out, grad_up, grad_down, grad_slice, grad_mix)


def solution(mesh):
    split = P(("design", "pts"), None)
    placed = (split, split, P(("design", "pts")), split) + (P(),) * 12
    return jax.shard_map(
        functools.partial(on_device, mesh.shape["pts"]),
        mesh=mesh,
        in_specs=placed,
        out_specs=(split,) * 6 + (P("design", None), P("design", None, None)),
        check_vma=False,
    )
```

```python
import functools
import math

import jax
import jax.numpy as jnp
from jax import lax
from jax.experimental import pallas as pl
from jax.experimental.pallas import tpu as pltpu
from jax.sharding import PartitionSpec as P

F32 = jnp.float32
BF16 = jnp.bfloat16
EPS = 1e-05
GROUP_BITS = (0, 2)
GELU_A = math.sqrt(2.0 / math.pi)
GELU_B = 0.044715

NN = ((1,), (0,))
NT = ((1,), (1,))
TN = ((0,), (0,))


def dot(left, right, dims=NN, precision=None):
    return lax.dot_general(
        left, right, (dims, ((), ())), precision=precision, preferred_element_type=F32
    )


def bit_reverse(value, bits):
    out = 0
    for k in range(bits):
        out = (out << 1) | ((value >> k) & 1)
    return out


def group_of(me):
    out = 0
    for k, bit in enumerate(GROUP_BITS):
        out |= ((me >> bit) & 1) << k
    return out


def from_position(pos, order):
    out = 0
    for i, bit in enumerate(order):
        out |= ((pos >> (len(order) - 1 - i)) & 1) << bit
    return out


def norm_parts(inputs):
    centre = jnp.mean(inputs, axis=-1, keepdims=True)
    shifted = inputs - centre
    spread = jnp.mean(shifted * shifted, axis=-1, keepdims=True)
    return shifted, lax.rsqrt(spread + EPS)


def pad_to(count, unit):
    return -(-count // unit) * unit


def split(value):
    high = value.astype(BF16)
    return high, (value - high.astype(F32)).astype(BF16)


def narrow_dot(left, right):
    left_high, left_low = split(left)
    right_high, right_low = split(right)
    return dot(
        jnp.concatenate([left_high, left_high, left_low], axis=0),
        jnp.concatenate([right_high, right_low, right_high], axis=0),
        TN,
    )


def wide_dot(left, right_parts, dims):
    rows = left.shape[0]
    high, low = split(left)
    right_high, right_low = right_parts
    both = dot(jnp.concatenate([high, low], axis=0), right_high, dims)
    return both[:rows] + both[rows:] + dot(high, right_low, dims)


def place_groups(value_of, keep, send, mine):
    half = keep.shape[0]
    bits = (2 * half).bit_length() - 1
    for pos in range(2 * half):
        target = keep if pos < half else send
        target[pos % half] = value_of(bit_reverse(pos, bits) ^ mine)


def sums_kernel(
    counts_hbm,
    sharpness_hbm,
    points_hbm,
    geometry_hbm,
    gain_hbm,
    w_feat_hbm,
    w_mid_hbm,
    w_slice_hbm,
    keep,
    send,
    normed_out,
    features_out,
    middle_out,
    weights_out,
    geo_weights_out,
    low_out,
    geo_low_out,
    total,
    maps,
    counts,
    sharpness,
    points,
    geometry,
    gain,
    w_feat,
    w_mid,
    w_slice,
    sems,
):
    copies = [
        pltpu.make_async_copy(source, target, sems.at[i])
        for i, (source, target) in enumerate(
            (
                (points_hbm, points),
                (geometry_hbm, geometry),
                (w_feat_hbm, w_feat),
                (w_mid_hbm, w_mid),
                (gain_hbm, gain),
                (w_slice_hbm, w_slice),
                (sharpness_hbm, sharpness),
                (counts_hbm, counts),
            )
        )
    ]
    for copy in copies:
        copy.start()
    me = lax.axis_index("pts")
    rows, model = points.shape
    all_rows = rows + geometry.shape[0]
    width, slices = w_slice.shape
    heads = model // width
    groups = total.shape[0]
    per = heads // groups
    lanes = math.gcd(rows, 128)
    filled = 2 * per * (width + 1)
    total[:, filled:, :] = jnp.zeros((groups, total.shape[1] - filled, slices), F32)
    for copy in copies:
        copy.wait()
    slice_t = w_slice[...].T
    maps[:model, :] = w_feat[...].T
    maps[model:, :] = w_mid[...].T
    gain_column = jnp.broadcast_to(gain[...].reshape(1, model), (8, model)).T[:, :1]
    live = lax.broadcasted_iota(jnp.int32, (1, rows), 1) < counts[0]
    blocks = range(0, all_rows, rows)
    for start in blocks:
        at = slice(start, start + rows)
        inputs = points[...] if start == 0 else geometry[start - rows : start, :]
        inputs_t = inputs.T.astype(F32)
        shifted = inputs_t - jnp.mean(inputs_t, axis=0, keepdims=True)
        scale = lax.rsqrt(jnp.mean(shifted * shifted, axis=0, keepdims=True) + EPS)
        normed = (shifted * scale * gain_column).astype(BF16)
        both = dot(maps[...], normed).astype(BF16)
        normed_out[:, at] = normed
        features_out[:, at] = both[:model]
        middle_out[:, at] = both[model:]

    def logits_of(h):
        own = slice(h * width, (h + 1) * width)
        return [dot(slice_t, middle_out[own, start : start + rows]) for start in blocks]

    def numerators(h):
        own = slice(h * width, (h + 1) * width)
        cols = slice(h * slices, (h + 1) * slices)
        g, j = h // per, h % per
        for geo, (low_ref, at) in enumerate(
            ((low_out, slice(0, rows)), (geo_low_out, slice(rows, all_rows)))
        ):
            row = (geo * per + j) * width
            total[g, row : row + width, :] = dot(features_out[own, at], low_ref[cols, :], NT)

    ahead = logits_of(0)
    for h in range(heads):
        cols = slice(h * slices, (h + 1) * slices)
        logits = ahead
        if h + 1 < heads:
            ahead = logits_of(h + 1)
        factor = sharpness[h] * math.log2(math.e)
        for geo, first in ((0, 0), (1, 1)):
            weights_ref, low_ref = ((weights_out, low_out), (geo_weights_out, geo_low_out))[geo]
            folded = None
            for i in range(first, 1 if geo == 0 else len(logits)):
                for start in range(0, rows, lanes):
                    part = logits[i][:, start : start + lanes]
                    powers = jnp.exp2((part - jnp.max(part, axis=0, keepdims=True)) * factor)
                    inverse = 1.0 / jnp.sum(powers, axis=0, keepdims=True)
                    if geo == 0:
                        inverse = jnp.where(live[:, start : start + lanes], inverse, 0.0)
                    weights = powers * inverse
                    where = (i - first) * rows + start
                    weights_ref[cols, where : where + lanes] = weights
                    low_ref[cols, where : where + lanes] = weights.astype(BF16)
                    folded = weights if folded is None else folded + weights
            row = 2 * per * width + geo * per + h % per
            total[h // per, row : row + 1, :] = jnp.sum(folded.T, axis=0, keepdims=True)
        if h > 0:
            numerators(h - 1)
    numerators(heads - 1)

    place_groups(lambda g: total[g], keep, send, group_of(me))


tie = lax.optimization_barrier


def token_rows(tokens, j, per, width):
    base = 2 * per * width
    out = []
    for geo in range(2):
        row = (geo * per + j) * width
        den = tokens[base + geo * per + j : base + geo * per + j + 1, :] + EPS
        out.append((tokens[row : row + width, :] / den, den))
    return out


def mix_kernel(tokens, w_query, w_key, w_value, mixed_out, attention_out, kept):
    width = w_query.shape[0]
    per = attention_out.shape[0]
    slices = tokens.shape[1]
    maps = jnp.concatenate([w_query[...], w_key[...], w_value[...]], axis=1)
    heads = range(per)
    both = [
        jnp.concatenate([part for part, _ in token_rows(tokens, j, per, width)], axis=1)
        for j in heads
    ]
    projected = [narrow_dot(maps, both[j]) for j in heads]
    for j in heads:
        kept[j] = projected[j]
    scores = [narrow_dot(projected[j][width : 2 * width], projected[j][:width, :slices]) for j in heads]
    attention = []
    for j in heads:
        scaled = (scores[j] - jnp.max(scores[j], axis=0, keepdims=True)) * (
            math.log2(math.e) / math.sqrt(width)
        )
        powers = jnp.exp2(scaled)
        attention.append(powers * (1.0 / jnp.sum(powers, axis=0, keepdims=True)))
    for j in heads:
        attention_out[j] = attention[j]
        mixed_out[j * width : (j + 1) * width, :] = wide_dot(
            projected[j][2 * width :], split(attention[j]), NN
        )


def mix_back_kernel(tokens, attention_in, kept, grad, w_query, w_key, w_value, out):
    width = w_query.shape[0]
    per, both_count, slices = attention_in.shape
    base = 2 * per * width
    small = jnp.zeros((width, 3 * width), F32)
    out[base : base + pad_to(2 * per, 8), :] = jnp.zeros((pad_to(2 * per, 8), slices), F32)
    maps_t = jnp.concatenate([w_query[...].T, w_key[...].T, w_value[...].T], axis=0)
    none = jnp.zeros((width, both_count - slices), F32)
    heads = range(per)
    rows = [token_rows(tokens, j, per, width) for j in heads]
    both = [jnp.concatenate([part for part, _ in rows[j]], axis=1) for j in heads]
    mixed_grads = [grad[j * width : (j + 1) * width, :] for j in heads]
    att_grads = [narrow_dot(kept[j, 2 * width :, :], mixed_grads[j]) for j in heads]
    value_grads = [wide_dot(mixed_grads[j], split(attention_in[j]), NT) for j in heads]
    score_grads = []
    for j in heads:
        attention = attention_in[j]
        inner = jnp.sum(attention * att_grads[j], axis=0, keepdims=True)
        score_grads.append(split(attention * (att_grads[j] - inner) * (1.0 / math.sqrt(width))))
    query_grads = [wide_dot(kept[j, width : 2 * width, :], score_grads[j], NN) for j in heads]
    key_grads = [wide_dot(kept[j, :width, :slices], score_grads[j], NT) for j in heads]
    grads = [
        jnp.concatenate(
            [jnp.concatenate([query_grads[j], none], axis=1), key_grads[j], value_grads[j]], axis=0
        )
        for j in heads
    ]
    both_grads = [narrow_dot(maps_t, grads[j]) for j in heads]
    for j in heads:
        small += wide_dot(both[j], split(grads[j]), NT)
        for g, (value_of, den) in enumerate(rows[j]):
            row = (g * per + j) * width
            scaled = both_grads[j][:, g * slices : (g + 1) * slices] / den
            out[row : row + width, :] = scaled
            out[base + g * per + j : base + g * per + j + 1, :] = -jnp.sum(
                scaled * value_of, axis=0, keepdims=True
            )
    half = width // 2
    filler = jnp.zeros((width, slices // 2 - 3 * width), F32)
    wide = jnp.concatenate([small, filler], axis=1)
    out[out.shape[0] - half :, :] = jnp.concatenate([wide[:half], wide[half:]], axis=1)


def mlp_kernel(
    rel,
    *refs,
):
    groups = len(rel)
    pieces = refs[:groups]
    (
        low,
        points,
        cotangent,
        w_out,
        gain,
        w_up,
        w_down,
        layer_out,
        grad_att_out,
        keep,
        send,
        attended,
        second_out,
        hidden_out,
        grad_upper_out,
        grad_resid_out,
        canon,
    ) = refs[groups:]
    me = lax.axis_index("pts")
    model = points.shape[1]
    slices = canon.shape[2]
    heads = low.shape[0] // slices
    width = model // heads
    per = heads // groups
    mine = group_of(me)
    for r, piece in zip(rel, pieces):
        canon[mine ^ r] = piece[...]
    for h in range(heads):
        cols = slice(h * slices, (h + 1) * slices)
        j = h % per
        attended[h * width : (h + 1) * width, :] = dot(
            canon[h // per, j * width : (j + 1) * width, :].astype(BF16), low[cols, :]
        ).astype(BF16)
    gain_row = gain[...].reshape(1, model)
    residual = points[...].astype(F32) + dot(attended[...], w_out[...], TN)
    shifted, scale = norm_parts(residual)
    unit = shifted * scale
    second = (unit * gain_row).astype(BF16)
    second_out[...] = second
    upper = dot(second, w_up[...])
    square = upper * upper
    slope = jnp.tanh(GELU_A * upper * (1.0 + GELU_B * square))
    half = 0.5 * (1.0 + slope)
    hidden = (upper * half).astype(BF16)
    hidden_out[...] = hidden
    curve = half + 0.5 * upper * (1.0 - slope * slope) * (
        GELU_A * (1.0 + 3.0 * GELU_B * square)
    )
    layer_out[...] = (residual + dot(hidden, w_down[...])).astype(BF16)
    grad_upper = (dot(cotangent[...], w_down[...], NT) * curve).astype(BF16)
    grad_upper_out[...] = grad_upper
    grad_unit = dot(grad_upper, w_up[...], NT) * gain_row
    grad_norm = scale * (
        grad_unit
        - jnp.mean(grad_unit, axis=-1, keepdims=True)
        - unit * jnp.mean(grad_unit * unit, axis=-1, keepdims=True)
    )
    grad_resid = (cotangent[...].astype(F32) + grad_norm).astype(BF16)
    grad_resid_out[...] = grad_resid
    grad_att = dot(w_out[...], grad_resid, NT).astype(BF16)
    grad_att_out[...] = grad_att
    for h in range(heads):
        j = h % per
        canon[h // per, j * width : (j + 1) * width, :] = dot(
            grad_att[h * width : (h + 1) * width], low[h * slices : (h + 1) * slices, :], NT
        )
    place_groups(lambda g: canon[g], keep, send, mine)


def outer_kernel(
    order, attended, second, hidden, grad_upper, grad_resid, cotangent, keep, send, out, up, down
):
    me = lax.axis_index("pts")
    half, rows, model = keep.shape
    parts = 2 * half
    step = model // parts
    wide = hidden.shape[1] // model
    out[...] = dot(attended[...], grad_resid[...])
    up[...] = dot(second[...], grad_upper[...], TN)
    down[...] = dot(hidden[...], cotangent[...], TN)
    for pos in range(parts):
        target = keep if pos < half else send
        p = from_position(pos, order) ^ me
        i = pos % half
        at = pl.ds(pl.multiple_of(p * step, step), step)
        target[i, :step, :] = out[at, :]
        for w in range(wide):
            target[i, step * (1 + w) : step * (2 + w), :] = up[at, w * model : (w + 1) * model]
        tall = step * wide
        target[i, step * (1 + wide) :, :] = down[pl.ds(pl.multiple_of(p * tall, tall), tall), :]


def back_kernel(rel, order, sharpness, *refs):
    groups = len(rel)
    pieces = refs[:groups]
    mixed = refs[groups : 2 * groups]
    (
        weights,
        geo_weights,
        low,
        geo_low,
        features,
        middle,
        normed,
        grad_att,
        w_slice,
        keep,
        send,
        grad_mix,
        canon,
        mix_canon,
        left_field,
        left_geo,
        low_numer,
        right,
        total,
        slice_sum,
        logit,
    ) = refs[2 * groups :]
    me = lax.axis_index("pts")
    model, rows = grad_att.shape
    width, slices = w_slice.shape
    heads = model // width
    per = heads // groups
    mine = group_of(me)
    base = 2 * per * width
    for r, piece, mix_piece in zip(rel, pieces, mixed):
        canon[mine ^ r] = piece[...]
        mix_canon[mine ^ r] = mix_piece[...]
    for h in range(heads):
        g, j = h // per, h % per
        for geo in range(2):
            row = (geo * per + j) * width
            numer = canon[g, row : row + width, :].astype(BF16)
            low_numer[geo, h * width : (h + 1) * width, :] = numer
            den = canon[g, base + geo * per + j : base + geo * per + j + 1, :]
            high = den.astype(BF16).astype(F32)
            middle_part = (den - high).astype(BF16).astype(F32)
            rest = den - high - middle_part
            den_rows = jnp.concatenate([high, middle_part, rest, jnp.zeros((13, slices), F32)], axis=0)
            parts = [numer.astype(F32)]
            if not geo:
                parts.append(mix_canon[g, j * width : (j + 1) * width, :])
            parts.append(den_rows)
            left = jnp.concatenate(parts, axis=0).astype(BF16).T
            if geo:
                left_geo[h] = left
            else:
                left_field[h] = left
    all_rows = normed.shape[1]
    lanes = math.gcd(rows, 128)
    ones = jnp.ones((16, rows), BF16)
    blocks = range(0, all_rows, rows)

    def products_of(h):
        own = slice(h * width, (h + 1) * width)
        out = []
        for start in blocks:
            stack = [features[own, start : start + rows]]
            if start == 0:
                stack.append(grad_att[own, :])
            left = left_field if start == 0 else left_geo
            out.append(dot(left[h], jnp.concatenate(stack + [ones], axis=0)))
        return out

    def finish(h):
        cols = slice(h * slices, (h + 1) * slices)
        own = slice(h * width, (h + 1) * width)
        right[own, :rows] = dot(low_numer[0, own, :], low[cols, :]).astype(BF16)
        right[own, rows:] = dot(low_numer[1, own, :], geo_low[cols, :]).astype(BF16)
        right[model + h * width : model + (h + 1) * width, :] = dot(
            w_slice[...], logit[cols, :]
        ).astype(BF16)
        term = dot(logit[cols, :], middle[own, :], NT)
        if h == 0:
            slice_sum[...] = term
        else:
            slice_sum[...] += term

    ahead = products_of(0)
    for h in range(heads):
        cols = slice(h * slices, (h + 1) * slices)
        products = ahead
        if h + 1 < heads:
            ahead = products_of(h + 1)
        for i, begin in enumerate(blocks):
            for start in range(0, rows, lanes):
                grad_weights = products[i][:, start : start + lanes]
                if i == 0:
                    share = weights[cols, start : start + lanes]
                else:
                    where = begin - rows + start
                    share = geo_weights[cols, where : where + lanes]
                inner = jnp.sum(share * grad_weights, axis=0, keepdims=True)
                logit[cols, begin + start : begin + start + lanes] = (
                    share * (grad_weights - inner) * sharpness[h]
                ).astype(BF16)
        if h > 0:
            finish(h - 1)
    finish(heads - 1)

    total[...] = dot(normed[...], right[...], NT)
    half = keep.shape[0] // 2
    step = model // (2 * half)
    for pos in range(2 * half):
        start = pl.multiple_of((from_position(pos, order) ^ me) * step, step)
        value = total[pl.ds(start, step), :]
        if pos < half:
            keep[2 * pos] = value[:, :model]
            keep[2 * pos + 1] = value[:, model:]
        else:
            row = (pos - half) * 2 * step
            send[row : row + step, :] = value[:, :model]
            send[row + step : row + 2 * step, :] = value[:, model:]
    send[half * 2 * step :, :] = slice_sum[...].T

    small_rows = width // 2
    packed = canon[0, canon.shape[1] - small_rows :, :]
    for g in range(1, groups):
        packed += canon[g, canon.shape[1] - small_rows :, :]
    wide = jnp.concatenate([packed[:, : slices // 2], packed[:, slices // 2 :]], axis=0)
    for i in range(3):
        grad_mix[i] = wide[:, i * width : (i + 1) * width]


def add_kernel(left, right, out):
    out[...] = left[...] + right[...]


def finish_kernel(keep, got, slice_sum, feat, mid, slice_out):
    step = feat.shape[0]
    feat[...] = keep[:step, :] + got[:step, :]
    mid[...] = keep[step:, :] + got[step : 2 * step, :]
    slice_out[...] = slice_sum[...] + got[2 * step :, :]


def place_kernel(value, out, up, down):
    step, model = out.shape
    wide = up.shape[1] // model
    out[...] = value[0, :step, :]
    for w in range(wide):
        up[:, w * model : (w + 1) * model] = value[0, step * (1 + w) : step * (2 + w), :]
    down[...] = value[0, step * (1 + wide) :, :]


VMEM = pl.BlockSpec(memory_space=pltpu.VMEM)
SMEM = pl.BlockSpec(memory_space=pltpu.SMEM)
HBM = pl.BlockSpec(memory_space=pltpu.HBM)
MIB = 1024 * 1024
COSTS = {"point_back": 0.5, "mix_back": 0.001, "add": 12.0}


def shape(dims, dtype=F32):
    return jax.ShapeDtypeStruct(tuple(dims), dtype)


def run(body, name, limit, first, out_shape, scratch, *args):
    estimate = None
    if name in COSTS:
        estimate = pl.CostEstimate(
            flops=int(COSTS[name] * 1e9), bytes_accessed=0, transcendentals=0
        )
    rest = HBM if first is HBM else VMEM
    if first is HBM:
        args = args[:1] + tuple(
            pltpu.with_memory_space_constraint(arg, pltpu.HBM) for arg in args[1:]
        )
    return pl.pallas_call(
        body,
        out_shape=out_shape,
        in_specs=[first] + [rest] * (len(args) - 1),
        out_specs=jax.tree.map(lambda _: VMEM, out_shape),
        scratch_shapes=scratch,
        compiler_params=pltpu.CompilerParams(vmem_limit_bytes=limit * MIB),
        name=name,
        cost_estimate=estimate,
    )(*args)


def on_device(
    parts,
    points,
    geometry,
    counts,
    cotangent,
    gain_attn,
    w_feat,
    w_mid,
    w_slice,
    sharpness,
    w_query,
    w_key,
    w_value,
    w_out,
    gain_mlp,
    w_up,
    w_down,
):
    rows, model = points.shape
    geo_rows = geometry.shape[0]
    all_rows = rows + geo_rows
    width, slices = w_slice.shape
    heads = sharpness.shape[0]
    hidden_width = w_up.shape[1]
    all_bits = parts.bit_length() - 1
    bits = len(GROUP_BITS)
    rest_bits = [bit for bit in range(all_bits) if bit not in GROUP_BITS]
    groups = 1 << bits
    per = heads // groups
    token_height = 2 * per * width + pad_to(2 * per, 8)
    grad_height = token_height + width // 2
    half = groups // 2
    step = model // parts
    wide = hidden_width // model

    def exchange(value, bit):
        return lax.ppermute(value, "pts", [(i, i ^ (1 << bit)) for i in range(parts)])

    def fold(keep, got):
        count = keep.shape[0] // 2
        return keep[:count] + got[:count], keep[count:] + got[count:]

    def add_all(value, over):
        for bit in over:
            value = value + exchange(value, bit)
        return value

    def collect(pieces):
        for bit in reversed(GROUP_BITS):
            pieces = pieces + [exchange(piece, bit) for piece in pieces]
        return pieces

    main_order = outer_order = tuple(range(all_bits))
    rel = [0]
    for bit in reversed(range(bits)):
        rel = rel + [r ^ (1 << bit) for r in rel]

    keep, send, normed, features, middle, weights, geo_weights, low, geo_low = run(
        sums_kernel,
        "slice_sums",
        20,
        HBM,
        (
            shape((half, token_height, slices)),
            shape((half, token_height, slices)),
            shape((model, all_rows), BF16),
            shape((model, all_rows), BF16),
            shape((model, all_rows), BF16),
            shape((heads * slices, rows)),
            shape((heads * slices, geo_rows)),
            shape((heads * slices, rows), BF16),
            shape((heads * slices, geo_rows), BF16),
        ),
        [
            pltpu.VMEM((groups, token_height, slices), F32),
            pltpu.VMEM((2 * model, model), BF16),
            pltpu.SMEM(counts.shape, jnp.int32),
            pltpu.SMEM(sharpness.shape, F32),
            pltpu.VMEM(points.shape, BF16),
            pltpu.VMEM(geometry.shape, BF16),
            pltpu.VMEM(gain_attn.shape, F32),
            pltpu.VMEM(w_feat.shape, BF16),
            pltpu.VMEM(w_mid.shape, BF16),
            pltpu.VMEM(w_slice.shape, BF16),
            pltpu.SemaphoreType.DMA((8,)),
        ],
        counts,
        sharpness,
        points,
        geometry,
        gain_attn,
        w_feat,
        w_mid,
        w_slice,
    )
    got = exchange(send, GROUP_BITS[0])
    for bit in GROUP_BITS[1:]:
        keep, send = fold(keep, got)
        got = exchange(send, bit)
    tokens = add_all((keep + got)[0], rest_bits)
    mixed, attention, kept = run(
        mix_kernel,
        "mix_tokens",
        12,
        VMEM,
        (
            shape((per * width, slices)),
            shape((per, 2 * slices, slices)),
            shape((per, 3 * width, 2 * slices)),
        ),
        [],
        tokens,
        w_query,
        w_key,
        w_value,
    )
    mixed_pieces = collect([mixed])
    (
        layer_out,
        grad_att,
        keep,
        send,
        attended,
        second,
        hidden,
        grad_upper,
        grad_resid,
    ) = run(
        functools.partial(mlp_kernel, tuple(rel)),
        "mlp",
        24,
        VMEM,
        (
            shape((rows, model), BF16),
            shape((model, rows), BF16),
            shape((half, per * width, slices)),
            shape((half, per * width, slices)),
            shape((model, rows), BF16),
            shape((rows, model), BF16),
            shape((rows, hidden_width), BF16),
            shape((rows, hidden_width), BF16),
            shape((rows, model), BF16),
        ),
        [pltpu.VMEM((groups, per * width, slices), F32)],
        *mixed_pieces,
        low,
        points,
        cotangent,
        w_out,
        gain_mlp,
        w_up,
        w_down,
    )
    got = exchange(send, GROUP_BITS[0])
    attended, second, hidden, grad_upper, grad_resid, got = tie(
        (attended, second, hidden, grad_upper, grad_resid, got)
    )
    outer_keep, outer_send = run(
        functools.partial(outer_kernel, outer_order),
        "weight_grads",
        16,
        VMEM,
        (shape((parts // 2, step * (1 + 2 * wide), model)),) * 2,
        [
            pltpu.VMEM((model, model), F32),
            pltpu.VMEM((model, hidden_width), F32),
            pltpu.VMEM((hidden_width, model), F32),
        ],
        attended,
        second,
        hidden,
        grad_upper,
        grad_resid,
        cotangent,
    )
    for bit in GROUP_BITS[1:]:
        keep, send = fold(keep, got)
        got = exchange(send, bit)
    outer_got = exchange(outer_send, outer_order[0])
    mixed_grad = add_all((keep + got)[0], rest_bits[:1])
    mixed_grad, outer_got = tie((mixed_grad, outer_got))
    outer_keep, outer_send = fold(outer_keep, outer_got)
    outer_got = exchange(outer_send, outer_order[1])
    mixed_grad = add_all(mixed_grad, rest_bits[1:])
    token_grad = run(
        mix_back_kernel,
        "mix_back",
        16,
        VMEM,
        shape((grad_height, slices)),
        [],
        tokens,
        attention,
        kept,
        mixed_grad,
        w_query,
        w_key,
        w_value,
    )
    grad_pieces = collect([token_grad])
    outer_keep, outer_send = fold(outer_keep, outer_got)
    outer_got = exchange(outer_send, outer_order[2])
    keep, send, grad_mix = run(
        functools.partial(back_kernel, tuple(rel), main_order),
        "point_back",
        24,
        SMEM,
        (
            shape((parts, step, model)),
            shape((parts * step + width, model)),
            shape((3, width, width)),
        ),
        [
            pltpu.VMEM((groups, grad_height, slices), F32),
            pltpu.VMEM((groups, per * width, slices), F32),
            pltpu.VMEM((heads, slices, 2 * width + 16), BF16),
            pltpu.VMEM((heads, slices, width + 16), BF16),
            pltpu.VMEM((2, model, slices), BF16),
            pltpu.VMEM((2 * model, all_rows), BF16),
            pltpu.VMEM((model, 2 * model), F32),
            pltpu.VMEM((slices, width), F32),
            pltpu.VMEM((heads * slices, all_rows), BF16),
        ],
        sharpness,
        *grad_pieces,
        *mixed_pieces,
        weights,
        geo_weights,
        low,
        geo_low,
        features,
        middle,
        normed,
        grad_att,
        w_slice,
    )
    keep = keep.reshape(-1, model)
    slice_sum = send[keep.shape[0] :]
    for turn, bit in enumerate(main_order):
        if turn == 0:
            send, outer_got = tie((send, outer_got))
            outer_keep, outer_send = fold(outer_keep, outer_got)
            outer_got = exchange(outer_send, outer_order[3])
        if turn == all_bits - 1:
            for late in outer_order[4:]:
                outer_keep, outer_send = fold(outer_keep, outer_got)
                outer_got = exchange(outer_send, late)
            outer = run(
                add_kernel, "add", 4, VMEM, shape(outer_keep.shape), [], outer_keep, outer_got
            )
            send, outer = tie((send, outer))
        got = exchange(send, bit)
        if turn == all_bits - 1:
            break
        slice_sum = slice_sum + got[keep.shape[0] :]
        count = keep.shape[0] // 2
        send = jnp.concatenate([keep[count:] + got[count : 2 * count], slice_sum], axis=0)
        keep = keep[:count] + got[:count]
    grad_out, grad_up, grad_down = run(
        place_kernel,
        "place",
        4,
        VMEM,
        (shape((step, model)), shape((step, hidden_width)), shape((step * wide, model))),
        [],
        outer,
    )
    grad_feat, grad_mid, grad_slice = run(
        finish_kernel,
        "finish",
        4,
        VMEM,
        (shape((step, model)), shape((step, model)), shape((width, slices))),
        [],
        keep,
        got,
        slice_sum,
    )
    return (layer_out, grad_feat, grad_mid, grad_out, grad_up, grad_down, grad_slice, grad_mix)


def solution(mesh):
    split = P(("design", "pts"), None)
    placed = (split, split, P(("design", "pts")), split) + (P(),) * 12
    return jax.shard_map(
        functools.partial(on_device, mesh.shape["pts"]),
        mesh=mesh,
        in_specs=placed,
        out_specs=(split,) * 6 + (P("design", None), P("design", None, None)),
        check_vma=False,
    )
```
